32 devices in a mesh: days: 2 (over y), sta: 8 (over z, x), win: 2 (over core).
Axes of the slice: x: 2, y: 2, z: 4, core: 2. Of those that a mesh axis runs over, the one named last changes fastest.
Arguments:
- phases: bfloat16 [48, 2048, 16], P(('days', 'win'), 'sta'), parts along dimension 0, may hold values from -3.140625 to 3.140625
- window_valid: int32 [48], P('days'), parts along dimension 0, may hold values 0 or 1
- freq_taper: float32 [2048], replicated, may hold values from 0.1 to 1.9
- pair_mask: int32 [8, 8], replicated, may hold values from 0 to 1, as said below
Outputs:
- correlations: float32 [32, 16, 512], P(('days', 'sta'), None, 'win'), parts along dimension 0
The draws below stay inside these ranges and needn't reach their ends.
There are 2 independent parts, one for each index of `days`. The reference program is written for one: setup_inputs(seed, part) draws one part's arguments, and reference() takes and returns one part's arrays. A program takes and returns all parts, laid end to end along the dimension named above; an argument that names none is the same for every part. Nothing has to cross between parts.
Inputs may be any that keep to these rules, and one draw needn't show every extreme that they name: `pair_mask`: symmetric over the two block indices; every diagonal block is kept.
All inputs are finite; a program needn't handle non-finite values.
Results may differ from the reference program's by a relative error of at most 0.005.
Values may be sent and summed in bfloat16 or wider, within the bound.
No kernel may reach another device: no remote copies, remote signals or barrier semaphores. Data moves between devices by JAX's collectives and lax.ppermute only.
A program may use at most 64 MiB of HBM per device.

```python
import math
import jax
import jax.numpy as jnp
from jax import lax

F = 2048
LAGS = 512
WL = 12
SDEV = 2
WINDOWS = 24
STATIONS = 16
NBLK = 8
N_STA = 8
N_WIN = 2


def draw_pair_mask(key, part):
    raw_bits = jax.random.randint(key, (NBLK, NBLK), 0, 2).astype(jnp.int32)
    row_index = jnp.arange(NBLK, dtype=jnp.int32)[:, None]
    col_index = jnp.arange(NBLK, dtype=jnp.int32)[None, :]
    symmetric = jnp.where(row_index <= col_index, raw_bits, raw_bits.T)
    return jnp.where(row_index == col_index, 1, symmetric).astype(jnp.int32)


def place_ends(result, own_key, least, largest):
    spot = [jax.random.randint(jax.random.fold_in(own_key, axis), (), 0, length) for axis, length in enumerate(result.shape)]
    widest = result.shape.index(max(result.shape))
    beside = spot[:widest] + [(spot[widest] + 1) % result.shape[widest]] + spot[widest + 1:]
    return result.at[tuple(spot)].set(least).at[tuple(beside)].set(largest)


def setup_inputs(seed: int = 0, part: int = 0) -> dict:
    splits = jax.random.split(jax.random.key(seed), 5)
    part_keys = jax.random.split(jax.random.fold_in(splits[4], part), 5)
    phases = jnp.clip(jax.random.uniform(part_keys[0], (WINDOWS, F, STATIONS), jnp.float32, -3.140625, 3.140625), -3.140625, 3.140625).astype(jnp.bfloat16)
    window_valid = place_ends((jax.random.randint(part_keys[1], (WINDOWS,), 0, 4) < 3).astype(jnp.int32), jax.random.fold_in(part_keys[1], 1), 0, 1)
    freq_taper = jnp.clip(1.0 + 0.18 * jax.random.normal(splits[2], (F,), jnp.float32), 0.1, 1.9)
    pair_mask = draw_pair_mask(jax.random.fold_in(splits[4], 71), part)
    return {"phases": phases, "window_valid": window_valid, "freq_taper": freq_taper, "pair_mask": pair_mask}


def lag_table(freq_bins, lag_count):
    freq_index = jnp.arange(freq_bins, dtype=jnp.int32)[:, None]
    lag_index = jnp.arange(lag_count, dtype=jnp.int32)[None, :] - lag_count // 2
    wrapped = jnp.mod(freq_index * lag_index, 2 * freq_bins)
    angle = wrapped.astype(jnp.float32) * (math.pi / freq_bins)
    return jnp.stack((jnp.cos(angle), -jnp.sin(angle))).astype(jnp.bfloat16)

def rounded(values):
    return lax.optimization_barrier(values.astype(jnp.bfloat16)).astype(jnp.float32)

def reference(phases, window_valid, freq_taper, pair_mask):
    phase_f = phases.astype(jnp.float32)
    phasor_cos = rounded(jnp.cos(phase_f)).reshape(N_WIN, WL, F, STATIONS)
    phasor_sin = rounded(jnp.sin(phase_f)).reshape(N_WIN, WL, F, STATIONS)
    valid_f = window_valid.astype(jnp.float32)
    valid_count = jnp.sum(valid_f)
    norm_scale = 1.0 / jnp.sqrt(F * jnp.maximum(valid_count, 1.0))
    valid_groups = valid_f.reshape(N_WIN, WL)[:, :, None, None]
    weighted_cos = phasor_cos * valid_groups
    weighted_sin = phasor_sin * valid_groups
    bin_weight = freq_taper.astype(jnp.float32) * norm_scale
    lag_f = lag_table(F, LAGS).astype(jnp.float32)
    keep_full = jnp.repeat(jnp.repeat(pair_mask, SDEV, 0), SDEV, 1).astype(jnp.float32)
    keep_full = keep_full * (1.0 - jnp.eye(STATIONS, dtype=jnp.float32))
    highest = lax.Precision.HIGHEST

    def one_block(index):
        start = index * SDEV
        recv_cos = lax.dynamic_slice_in_dim(weighted_cos, start, SDEV, 3)
        recv_sin = lax.dynamic_slice_in_dim(weighted_sin, start, SDEV, 3)
        cross_re = jnp.einsum('gwki,gwkj->gijk', recv_cos, phasor_cos, precision=highest)
        cross_re = cross_re + jnp.einsum('gwki,gwkj->gijk', recv_sin, phasor_sin, precision=highest)
        cross_im = jnp.einsum('gwki,gwkj->gijk', recv_sin, phasor_cos, precision=highest)
        cross_im = cross_im - jnp.einsum('gwki,gwkj->gijk', recv_cos, phasor_sin, precision=highest)
        spec_re = lax.optimization_barrier(jnp.sum(rounded(cross_re * bin_weight), axis=0))
        spec_im = lax.optimization_barrier(jnp.sum(rounded(cross_im * bin_weight), axis=0))
        stacked = jnp.stack((spec_re, spec_im))
        correlation = jnp.einsum('cijk,ckt->ijt', stacked, lag_f, precision=highest)
        pair_keep = lax.dynamic_slice_in_dim(keep_full, start, SDEV, 0)
        return correlation * pair_keep[:, :, None]
    blocks = lax.map(one_block, jnp.arange(N_STA, dtype=jnp.int32))
    return blocks.reshape(STATIONS, STATIONS, LAGS)
```

```python
import functools
import math

import jax
import jax.numpy as jnp
from jax import lax
from jax.experimental import pallas as pl
from jax.experimental.pallas import tpu as pltpu
from jax.sharding import PartitionSpec as P

LAGS = 512
VMEM = pl.BlockSpec(memory_space=pltpu.VMEM)
SMEM = pl.BlockSpec(memory_space=pltpu.SMEM)
PARAMS = pltpu.CompilerParams(vmem_limit_bytes=48 * 1024 * 1024)

COS_COEF = (
    0.9999999890590218,
    -0.49999989101070386,
    0.041666489217381156,
    -0.001388780359807859,
    2.476988355752502e-05,
    -2.707903082088142e-07,
    1.724509174527214e-09,
)
SIN_COEF = (
    0.9999997571451633,
    -0.06534424613196173,
    0.001711441007161203,
    -2.461450561671638e-05,
    1.977699154629728e-07,
)


def cos_sin(angle):
    square = angle * angle
    cosine = COS_COEF[-1]
    for coef in COS_COEF[-2::-1]:
        cosine = cosine * square + coef
    sine = SIN_COEF[-1]
    for coef in SIN_COEF[-2::-1]:
        sine = sine * square + coef
    sine = sine * (angle - angle * square * (1.0 / math.pi**2))
    return cosine, sine


def full_distances(blocks):
    half = blocks // 2
    return [(step, step + half) for step in range(1, half)]


def position():
    return lax.axis_index("sta"), lax.axis_index("win")


def cross_kernel(blocks, valid_ref, taper_ref, own_ref, other_ref, *refs):
    cos_ref, sin_ref = refs[-2:]
    own_part, far_part, *full_parts = refs[:-2]
    sta, win = position()
    windows, stations, bins = own_ref.shape
    rows = stations // blocks
    count = jnp.float32(0)
    for w in range(2 * windows):
        count += valid_ref[w].astype(jnp.float32)
    if bins % 128:
        taper = taper_ref[...]
    else:
        taper = taper_ref[:, pl.ds(pl.multiple_of(sta * bins, 128), bins)]
    total = jnp.maximum(jnp.full((1, bins), count, jnp.float32), 1.0)
    weight = taper * (1.0 / jnp.sqrt(blocks * bins * total))
    for group, phase_ref in enumerate((own_ref, other_ref)):
        first = (win if group == 0 else 1 - win) * windows

        def phasors(w, carry, group=group, phase_ref=phase_ref, first=first):
            cosine, sine = cos_sin(phase_ref[w].astype(jnp.float32))
            usable = valid_ref[first + w].astype(jnp.float32)
            cos_ref[group * windows + w] = cosine.astype(jnp.bfloat16).astype(jnp.float32) * usable
            sin_ref[group * windows + w] = sine.astype(jnp.bfloat16).astype(jnp.float32) * usable
            return carry

        lax.fori_loop(0, windows, phasors, 0, unroll=4)
    is_first = win == 0

    def row_of(ref, w, row):
        return ref[w, pl.ds(row, 1), :]

    def whole(out_ref, block):
        for r in range(rows):
            row = block * rows + r

            def add(w, sums, row=row):
                real, imag = sums
                row_cos, row_sin = row_of(cos_ref, w, row), row_of(sin_ref, w, row)
                cosine, sine = cos_ref[w], sin_ref[w]
                real = real + (row_cos * cosine + row_sin * sine)
                imag = imag + (row_sin * cosine - row_cos * sine)
                return real, imag

            zero = jnp.zeros((stations, bins), jnp.float32)
            real, imag = lax.fori_loop(0, 2 * windows, add, (zero, zero), unroll=8)
            out_ref[0, r] = (real * weight).astype(jnp.bfloat16)
            out_ref[1, r] = (imag * weight).astype(jnp.bfloat16)

    def part(out_ref, block):
        for r in range(rows):
            row = block * rows + r

            def add(w, total, row=row):
                row_cos, row_sin = row_of(cos_ref, w, row), row_of(sin_ref, w, row)
                left = jnp.where(is_first, row_cos, row_sin)
                right = jnp.where(is_first, row_sin, -row_cos)
                return total + (left * cos_ref[w] + right * sin_ref[w])

            zero = jnp.zeros((stations, bins), jnp.float32)
            total = lax.fori_loop(0, 2 * windows, add, zero, unroll=8)
            out_ref[r] = (total * weight).astype(jnp.bfloat16)

    for out_ref, pair in zip(full_parts, full_distances(blocks)):
        whole(out_ref, sta ^ jnp.where(is_first, pair[0], pair[1]))
    part(far_part, sta ^ (blocks // 2))
    part(own_part, sta)


def table_kernel(blocks, bins, part_ref, full_ref, row_cos, row_sin):
    sta, win = position()
    wrap = 2 * blocks * bins
    columns = part_ref.shape[-1]
    half = columns // 2
    step = 16
    column = lax.broadcasted_iota(jnp.int32, (step, columns), 1)
    mine_low = win == 0
    lag = jnp.where(mine_low, column - half, jnp.where(column < half, column, column - columns))

    def phasor(index):
        wrapped = ((index + wrap // 2) & (wrap - 1)) - wrap // 2
        return cos_sin(wrapped.astype(jnp.float32) * (2.0 * math.pi / wrap))

    fine = lax.broadcasted_iota(jnp.int32, (step, columns), 0)
    fine_cos, fine_sin = phasor(fine * lag)
    steps = bins // step
    full = full_distances(blocks)

    def band_rows(block, store):
        for start in range(0, steps, 16):
            count = min(16, steps - start)
            coarse = block * bins + (start + fine) * step
            coarse_cos, coarse_sin = phasor(coarse * lag)
            row_cos[...] = coarse_cos
            row_sin[...] = coarse_sin

            def fill(a, carry, start=start):
                left_cos = row_cos[pl.ds(a, 1), :]
                left_sin = row_sin[pl.ds(a, 1), :]
                cosine = left_cos * fine_cos - left_sin * fine_sin
                sine = left_sin * fine_cos + left_cos * fine_sin
                store(pl.ds(pl.multiple_of((start + a) * step, step), step), cosine, -sine)
                return carry

            lax.fori_loop(0, count, fill, 0, unroll=2)

    for slot, pair in enumerate(full):

        def store_full(place, cosine, sine, slot=slot):
            full_ref[slot, 0, place, :] = cosine.astype(jnp.bfloat16)
            full_ref[slot, 1, place, :] = sine.astype(jnp.bfloat16)

        band_rows(sta ^ jnp.where(mine_low, pair[0], pair[1]), store_full)
    for slot, distance in enumerate((0, blocks // 2)):

        def store_part(place, cosine, sine, slot=slot):
            part_ref[slot, place, :] = jnp.where(mine_low, cosine, sine).astype(jnp.bfloat16)

        band_rows(sta ^ distance, store_part)


def lag_kernel(blocks, mask_ref, part_ref, full_ref, own_ref, far_ref, *refs):
    mine_ref, theirs_ref = refs[-2:]
    sta, _ = position()
    rows, stations, bins = own_ref.shape
    pairs = rows * stations
    half = mine_ref.shape[-1]

    def times(spectra, table):
        return jnp.dot(spectra.reshape(pairs, bins), table, preferred_element_type=jnp.float32)

    total = times(own_ref[...], part_ref[0]) + times(far_ref[...], part_ref[1])
    for slot, spectra_ref in enumerate(refs[:-2]):
        for c in range(2):
            total = total + times(spectra_ref[c], full_ref[slot, c])
    source = lax.broadcasted_iota(jnp.int32, (stations, half), 0)
    kept = jnp.zeros((stations, half), jnp.float32)
    for block in range(blocks):
        kept = jnp.where(source // rows == block, mask_ref[sta, block].astype(jnp.float32), kept)
    for r in range(rows):
        keep = jnp.where(source == sta * rows + r, 0.0, kept)
        mine_ref[r] = total[r * stations : (r + 1) * stations, :half] * keep
        theirs_ref[r] = total[r * stations : (r + 1) * stations, half:] * keep


def per_device(phases, window_valid, freq_taper, pair_mask):
    blocks = lax.axis_size("sta")
    windows, bins, stations = phases.shape
    rows = stations // blocks
    full = full_distances(blocks)
    swap = [(0, 1), (1, 0)]
    own = jnp.transpose(phases, (0, 2, 1))
    other = lax.ppermute(own, "win", swap)
    if bins % 128:
        taper = lax.dynamic_slice_in_dim(freq_taper, lax.axis_index("sta") * bins, bins)
    else:
        taper = freq_taper
    part_shape = jax.ShapeDtypeStruct((rows, stations, bins), jnp.bfloat16)
    full_shape = jax.ShapeDtypeStruct((2, rows, stations, bins), jnp.bfloat16)
    part_table, full_table = pl.pallas_call(
        functools.partial(table_kernel, blocks, bins),
        out_shape=(
            jax.ShapeDtypeStruct((2, bins, LAGS), jnp.bfloat16),
            jax.ShapeDtypeStruct((len(full), 2, bins, LAGS), jnp.bfloat16),
        ),
        out_specs=(VMEM, VMEM),
        scratch_shapes=[pltpu.VMEM((16, LAGS), jnp.float32)] * 2,
        compiler_params=PARAMS,
        name="lag_table",
    )()
    own_part, far_part, *full_parts = pl.pallas_call(
        functools.partial(cross_kernel, blocks),
        out_shape=[part_shape, part_shape] + [full_shape] * len(full),
        in_specs=[SMEM, VMEM, VMEM, VMEM],
        out_specs=[VMEM] * (2 + len(full)),
        scratch_shapes=[pltpu.VMEM((2 * windows, stations, bins), jnp.float32)] * 2,
        compiler_params=PARAMS,
        name="cross_spectra",
    )(window_valid, taper.reshape(1, -1), own, other)
    axes = ("sta", "win")
    both = [(2 * b + w, 2 * (b ^ (blocks // 2)) + w) for b in range(blocks) for w in range(2)]
    far_part = lax.ppermute(far_part, axes, both)
    arrived = []
    for spectra, pair in zip(full_parts, full):
        moves = [(2 * b + w, 2 * (b ^ pair[w]) + w) for b in range(blocks) for w in range(2)]
        arrived.append(lax.ppermute(spectra, axes, moves))
    half_shape = jax.ShapeDtypeStruct((rows, stations, LAGS // 2), jnp.float32)
    mine, theirs = pl.pallas_call(
        functools.partial(lag_kernel, blocks),
        out_shape=(half_shape, half_shape),
        in_specs=[SMEM] + [VMEM] * (4 + len(full)),
        out_specs=(VMEM, VMEM),
        compiler_params=PARAMS,
        name="lag_sums",
    )(pair_mask, part_table, full_table, own_part, far_part, *arrived)
    return mine + lax.ppermute(theirs, "win", swap)


def solution(mesh):
    return jax.shard_map(
        per_device,
        mesh=mesh,
        in_specs=(P(("days", "win"), "sta", None), P("days"), P(), P()),
        out_specs=P(("days", "sta"), None, "win"),
        check_vma=False,
    )
```

```python
import functools
import math

import jax
import jax.numpy as jnp
from jax import lax
from jax.experimental import pallas as pl
from jax.experimental.pallas import tpu as pltpu
from jax.sharding import PartitionSpec as P

LAGS = 512
VMEM = pl.BlockSpec(memory_space=pltpu.VMEM)
ANY = pl.BlockSpec(memory_space=pl.ANY)
PARAMS = pltpu.CompilerParams(vmem_limit_bytes=48 * 1024 * 1024)

COS_COEF = (
    0.9999999890590218,
    -0.49999989101070386,
    0.041666489217381156,
    -0.001388780359807859,
    2.476988355752502e-05,
    -2.707903082088142e-07,
    1.724509174527214e-09,
)
SIN_COEF = (
    0.9999997571451633,
    -0.06534424613196173,
    0.001711441007161203,
    -2.461450561671638e-05,
    1.977699154629728e-07,
)


def cos_sin(angle):
    square = angle * angle
    cosine = COS_COEF[-1]
    for coef in COS_COEF[-2::-1]:
        cosine = cosine * square + coef
    sine = SIN_COEF[-1]
    for coef in SIN_COEF[-2::-1]:
        sine = sine * square + coef
    sine = sine * (angle - angle * square * (1.0 / math.pi**2))
    return cosine, sine


def full_distances(blocks):
    half = blocks // 2
    return [(step, step + half) for step in range(1, half)]


def in_hbm(array):
    return pltpu.with_memory_space_constraint(array, pltpu.HBM)


def position():
    return lax.axis_index("sta"), lax.axis_index("win")


def store_phasors(w, phase, usable, cos_ref, sin_ref, sum_ref, gap_ref):
    cosine, sine = cos_sin(phase.astype(jnp.float32))
    cosine = cosine.astype(jnp.bfloat16).astype(jnp.float32) * usable
    sine = sine.astype(jnp.bfloat16).astype(jnp.float32) * usable
    cos_ref[w] = cosine
    sin_ref[w] = sine
    sum_ref[w] = cosine + sine
    gap_ref[w] = cosine - sine


def prepare_kernel(blocks, phase_hbm, valid_hbm, taper_hbm, mask_hbm, *refs):
    own, (usable_ref, weight_ref, keep_ref) = refs[:4], refs[4:7]
    phase_ref, valid_ref, taper_ref, mask_ref, sems = refs[7:]
    sta, win = position()
    windows, stations, bins = phase_ref.shape
    rows = stations // blocks
    if taper_hbm.shape[1] > bins:
        taper_hbm = taper_hbm.at[:, pl.ds(pl.multiple_of(sta * bins, 128), bins)]
    copies = [
        pltpu.make_async_copy(source, target, sems.at[c])
        for c, (source, target) in enumerate(
            (
                (phase_hbm, phase_ref),
                (valid_hbm, valid_ref),
                (taper_hbm, taper_ref),
                (mask_hbm, mask_ref),
            )
        )
    ]
    for copy in copies:
        copy.start()
    for copy in copies[1:]:
        copy.wait()
    count = jnp.float32(0)
    for w in range(2 * windows):
        count += valid_ref[w].astype(jnp.float32)
    total = jnp.maximum(jnp.full((1, bins), count, jnp.float32), 1.0)
    weight_ref[...] = taper_ref[...] * (1.0 / jnp.sqrt(blocks * bins * total))
    for w in range(windows):
        usable = valid_ref[(1 - win) * windows + w].astype(jnp.float32)
        usable_ref[w] = jnp.full((1, bins), usable, jnp.float32)
    source = lax.broadcasted_iota(jnp.int32, keep_ref.shape[1:], 0)
    kept = jnp.zeros(keep_ref.shape[1:], jnp.float32)
    for block in range(blocks):
        kept = jnp.where(source // rows == block, mask_ref[sta, block].astype(jnp.float32), kept)
    for r in range(rows):
        keep_ref[r] = jnp.where(source == sta * rows + r, 0.0, kept)
    copies[0].wait()

    def phasors(w, carry):
        usable = valid_ref[win * windows + w].astype(jnp.float32)
        store_phasors(w, phase_ref[w], usable, *own)
        return carry

    lax.fori_loop(0, windows, phasors, 0, unroll=4)


def part_sums(out_ref, block, is_first, groups, weight):
    rows, stations, bins = out_ref.shape
    totals = [jnp.zeros((stations, bins), jnp.float32)] * rows
    for cos_ref, sin_ref, *_ in groups:

        def add(w, totals, cos_ref=cos_ref, sin_ref=sin_ref):
            cosine, sine = cos_ref[w], sin_ref[w]
            added = []
            for r in range(rows):
                row_cos = cos_ref[w, pl.ds(block * rows + r, 1), :]
                row_sin = sin_ref[w, pl.ds(block * rows + r, 1), :]
                left = jnp.where(is_first, row_cos, row_sin)
                right = jnp.where(is_first, row_sin, -row_cos)
                added.append(totals[r] + (left * cosine + right * sine))
            return added

        totals = lax.fori_loop(0, cos_ref.shape[0], add, totals, unroll=6)
    for r in range(rows):
        out_ref[r] = (totals[r] * weight).astype(jnp.bfloat16)


def full_sums(out_ref, block, groups, weight):
    _, rows, stations, bins = out_ref.shape
    totals = [(jnp.zeros((stations, bins), jnp.float32),) * 3] * rows
    for cos_ref, sin_ref, sum_ref, gap_ref in groups:

        def add(w, totals, cos_ref=cos_ref, sin_ref=sin_ref, sum_ref=sum_ref, gap_ref=gap_ref):
            cosine, plus, gap = cos_ref[w], sum_ref[w], gap_ref[w]
            added = []
            for r in range(rows):
                row = pl.ds(block * rows + r, 1)
                both, left, right = totals[r]
                added.append(
                    (
                        both + sum_ref[w, row, :] * cosine,
                        left + sin_ref[w, row, :] * gap,
                        right + cos_ref[w, row, :] * plus,
                    )
                )
            return added

        totals = lax.fori_loop(0, cos_ref.shape[0], add, totals, unroll=6)
    for r in range(rows):
        both, left, right = totals[r]
        out_ref[0, r] = ((both - left) * weight).astype(jnp.bfloat16)
        out_ref[1, r] = ((both - right) * weight).astype(jnp.bfloat16)


def cross_kernel(blocks, phase_ref, usable_ref, weight_ref, *refs):
    own, other, (far_part, *full_parts) = refs[:4], refs[4:8], refs[8:]
    sta, win = position()
    is_first = win == 0

    def phasors(w, carry):
        store_phasors(w, phase_ref[w], usable_ref[w], *other)
        return carry

    lax.fori_loop(0, phase_ref.shape[0], phasors, 0, unroll=4)
    weight = weight_ref[...]
    for out_ref, pair in zip(full_parts, full_distances(blocks)):
        full_sums(out_ref, sta ^ jnp.where(is_first, pair[0], pair[1]), (own, other), weight)
    part_sums(far_part, sta ^ (blocks // 2), is_first, (own, other), weight)


def table_kernel(blocks, weight_ref, *refs):
    own, other, (own_part, part_ref, full_ref, row_cos, row_sin) = refs[:4], refs[4:8], refs[8:]
    sta, win = position()
    bins, columns = part_ref.shape[1:]
    wrap = 2 * blocks * bins
    half = columns // 2
    step = 16
    column = lax.broadcasted_iota(jnp.int32, (step, columns), 1)
    is_first = win == 0
    lag = jnp.where(is_first, column - half, jnp.where(column < half, column, column - columns))

    def phasor(index):
        wrapped = ((index + wrap // 2) & (wrap - 1)) - wrap // 2
        return cos_sin(wrapped.astype(jnp.float32) * (2.0 * math.pi / wrap))

    fine = lax.broadcasted_iota(jnp.int32, (step, columns), 0)
    fine_cos, fine_sin = phasor(fine * lag)
    steps = bins // step

    def band_rows(block, store):
        for start in range(0, steps, step):
            coarse = block * bins + (start + fine) * step
            row_cos[...], row_sin[...] = phasor(coarse * lag)

            def fill(a, carry, start=start):
                left_cos = row_cos[pl.ds(a, 1), :]
                left_sin = row_sin[pl.ds(a, 1), :]
                cosine = left_cos * fine_cos - left_sin * fine_sin
                sine = left_sin * fine_cos + left_cos * fine_sin
                store(pl.ds(pl.multiple_of((start + a) * step, step), step), cosine, -sine)
                return carry

            lax.fori_loop(0, min(step, steps - start), fill, 0, unroll=2)

    for slot, pair in enumerate(full_distances(blocks)):

        def store_full(place, cosine, sine, slot=slot):
            full_ref[slot, 0, place, :] = cosine.astype(jnp.bfloat16)
            full_ref[slot, 1, place, :] = sine.astype(jnp.bfloat16)

        band_rows(sta ^ jnp.where(is_first, pair[0], pair[1]), store_full)
    for slot, distance in enumerate((0, blocks // 2)):

        def store_part(place, cosine, sine, slot=slot):
            part_ref[slot, place, :] = jnp.where(is_first, cosine, sine).astype(jnp.bfloat16)

        band_rows(sta ^ distance, store_part)
    part_sums(own_part, sta, is_first, (own, other), weight_ref[...])


def times(spectra, table):
    pairs = spectra.shape[0] * spectra.shape[1]
    return jnp.dot(spectra.reshape(pairs, -1), table, preferred_element_type=jnp.float32)


def early_kernel(part_ref, full_ref, own_ref, *refs):
    total = times(own_ref[...], part_ref[0])
    for slot, spectra_ref in enumerate(refs[:-1]):
        for c in range(2):
            total = total + times(spectra_ref[c], full_ref[slot, c])
    refs[-1][...] = total


def late_kernel(side, keep_ref, part_ref, full_ref, early_ref, far_ref, last_ref, out_ref):
    rows, stations, half = out_ref.shape
    lags = pl.ds(side * half, half)
    total = early_ref[:, lags] + times(far_ref[...], part_ref[1, :, lags])
    slot = full_ref.shape[0] - 1
    for c in range(2):
        total = total + times(last_ref[c], full_ref[slot, c, :, lags])
    out_ref[...] = total.reshape(rows, stations, half) * keep_ref[...]


def per_device(phases, window_valid, freq_taper, pair_mask):
    blocks = lax.axis_size("sta")
    windows, bins, stations = phases.shape
    rows = stations // blocks
    half = LAGS // 2
    full = full_distances(blocks)
    swap = [(0, 1), (1, 0)]

    def kernel(body, name, outs, ins, scratch=()):
        return pl.pallas_call(
            body,
            out_shape=[jax.ShapeDtypeStruct(shape, dtype) for shape, dtype in outs],
            in_specs=ins,
            out_specs=[VMEM] * len(outs),
            scratch_shapes=list(scratch),
            compiler_params=PARAMS,
            name=name,
        )

    f32, bf16 = jnp.float32, jnp.bfloat16
    phasor_set = [((windows, stations, bins), f32)] * 4
    part_shape = ((rows, stations, bins), bf16)
    full_shape = ((2, rows, stations, bins), bf16)
    half_shape = ((rows, stations, half), f32)
    phases = jnp.transpose(phases, (0, 2, 1))
    arriving = lax.ppermute(phases, "win", swap)
    taper = freq_taper
    if bins % 128:
        taper = lax.dynamic_slice_in_dim(freq_taper, lax.axis_index("sta") * bins, bins)
    *own, usable, weight, keep = kernel(
        functools.partial(prepare_kernel, blocks),
        "own_phasors",
        phasor_set + [((windows, 1, bins), f32), ((1, bins), f32), half_shape],
        [ANY] * 4,
        [
            pltpu.VMEM((windows, stations, bins), bf16),
            pltpu.SMEM(window_valid.shape, jnp.int32),
            pltpu.VMEM((1, bins), f32),
            pltpu.SMEM(pair_mask.shape, jnp.int32),
            pltpu.SemaphoreType.DMA((4,)),
        ],
    )(*(in_hbm(array) for array in (phases, window_valid, taper.reshape(1, -1), pair_mask)))
    cross = kernel(
        functools.partial(cross_kernel, blocks),
        "cross_spectra",
        phasor_set + [part_shape] + [full_shape] * len(full),
        [VMEM] * 7,
    )(arriving, usable, weight, *own)
    other, far_part, full_parts = cross[:4], cross[4], cross[5:]
    axes = ("sta", "win")

    def send(spectra, pair):
        moves = [(2 * b + w, 2 * (b ^ pair[w]) + w) for b in range(blocks) for w in range(2)]
        return lax.ppermute(spectra, axes, moves)

    arrived = [send(spectra, pair) for spectra, pair in zip(full_parts, full)]
    far_part = send(far_part, (blocks // 2, blocks // 2))
    own_part, part_table, full_table = kernel(
        functools.partial(table_kernel, blocks),
        "lag_table",
        [part_shape, ((2, bins, LAGS), bf16), ((len(full), 2, bins, LAGS), bf16)],
        [VMEM] * 9,
        [pltpu.VMEM((16, LAGS), f32)] * 2,
    )(weight, *own, *other)
    (early,) = kernel(
        early_kernel,
        "lag_sums_early",
        [((rows * stations, LAGS), f32)],
        [VMEM] * (2 + len(full)),
    )(part_table, full_table, own_part, *arrived[:-1])

    def late(side):
        return kernel(
            functools.partial(late_kernel, side), "lag_sums_late", [half_shape], [VMEM] * 6
        )(keep, part_table, full_table, early, far_part, arrived[-1])[0]

    theirs = lax.ppermute(late(1), "win", swap)
    return late(0) + theirs


def solution(mesh):
    return jax.shard_map(
        per_device,
        mesh=mesh,
        in_specs=(P(("days", "win"), "sta", None), P("days"), P(), P()),
        out_specs=P(("days", "sta"), None, "win"),
        check_vma=False,
    )
```

```python
import functools
import math

import jax
import jax.numpy as jnp
from jax import lax
from jax.experimental import pallas as pl
from jax.experimental.pallas import tpu as pltpu
from jax.sharding import PartitionSpec as P

LAGS = 512
LATE = 2
CHAIN = True
RING = (1, 2, 0, 3)
SHIFTS = (3, 1, 2)
VMEM = pl.BlockSpec(memory_space=pltpu.VMEM)
ANY = pl.BlockSpec(memory_space=pl.ANY)
PARAMS = pltpu.CompilerParams(vmem_limit_bytes=48 * 1024 * 1024)

COS_COEF = (
    0.9999999890590218,
    -0.49999989101070386,
    0.041666489217381156,
    -0.001388780359807859,
    2.476988355752502e-05,
    -2.707903082088142e-07,
    1.724509174527214e-09,
)
SIN_COEF = (
    0.9999997571451633,
    -0.06534424613196173,
    0.001711441007161203,
    -2.461450561671638e-05,
    1.977699154629728e-07,
)


def cos_sin(angle):
    square = angle * angle
    cosine = COS_COEF[-1]
    for coef in COS_COEF[-2::-1]:
        cosine = cosine * square + coef
    sine = SIN_COEF[-1]
    for coef in SIN_COEF[-2::-1]:
        sine = sine * square + coef
    sine = sine * (angle - angle * square * (1.0 / math.pi**2))
    return cosine, sine


def rounds_of(blocks):
    pairs = blocks // 2
    ring, shifts = (RING, SHIFTS) if len(RING) == pairs else (range(pairs), range(1, pairs))
    place = {pair: index for index, pair in enumerate(ring)}

    def receivers(shift, flip):
        moved = [ring[(place[b // 2] + shift) % pairs] for b in range(blocks)]
        return tuple(2 * pair + (b % 2 ^ flip) for b, pair in enumerate(moved))

    rounds = [(True, (receivers(shift, 0), receivers(shift, 1))) for shift in shifts]
    return rounds + [(False, (receivers(0, 1), receivers(0, 1)))]


def lookup(values, sta):
    found = jnp.int32(values[0])
    for b, value in enumerate(values[1:], 1):
        found = jnp.where(sta == b, value, found)
    return found


def peer(targets, sta, is_first):
    return jnp.where(is_first, lookup(targets[0], sta), lookup(targets[1], sta))


def sources(targets):
    return tuple(tuple(sorted(range(len(side)), key=lambda b: side[b])) for side in targets)


def in_hbm(array):
    return pltpu.with_memory_space_constraint(array, pltpu.HBM)


def position():
    return lax.axis_index("sta"), lax.axis_index("win")


def store_phasors(w, phase, usable, cos_ref, sin_ref, sum_ref, gap_ref):
    cosine, sine = cos_sin(phase.astype(jnp.float32))
    cosine = cosine.astype(jnp.bfloat16).astype(jnp.float32) * usable
    sine = sine.astype(jnp.bfloat16).astype(jnp.float32) * usable
    cos_ref[w] = cosine
    sin_ref[w] = sine
    sum_ref[w] = cosine + sine
    gap_ref[w] = cosine - sine


def prepare_kernel(blocks, phase_hbm, valid_hbm, taper_hbm, mask_hbm, *refs):
    own, (usable_ref, weight_ref, keep_ref) = refs[:4], refs[4:7]
    phase_ref, valid_ref, taper_ref, mask_ref, sems = refs[7:]
    sta, win = position()
    windows, stations, bins = phase_ref.shape
    rows = stations // blocks
    if taper_hbm.shape[1] > bins:
        taper_hbm = taper_hbm.at[:, pl.ds(pl.multiple_of(sta * bins, 128), bins)]
    copies = [
        pltpu.make_async_copy(source, target, sems.at[c])
        for c, (source, target) in enumerate(
            (
                (phase_hbm, phase_ref),
                (valid_hbm, valid_ref),
                (taper_hbm, taper_ref),
                (mask_hbm, mask_ref),
            )
        )
    ]
    for copy in copies:
        copy.start()
    for copy in copies[1:]:
        copy.wait()
    count = jnp.float32(0)
    for w in range(2 * windows):
        count += valid_ref[w].astype(jnp.float32)
    total = jnp.maximum(jnp.full((1, bins), count, jnp.float32), 1.0)
    weight_ref[...] = taper_ref[...] * (1.0 / jnp.sqrt(blocks * bins * total))
    for w in range(windows):
        usable = valid_ref[(1 - win) * windows + w].astype(jnp.float32)
        usable_ref[w] = jnp.full((1, bins), usable, jnp.float32)
    source = lax.broadcasted_iota(jnp.int32, keep_ref.shape[1:], 0)
    kept = jnp.zeros(keep_ref.shape[1:], jnp.float32)
    for block in range(blocks):
        kept = jnp.where(source // rows == block, mask_ref[sta, block].astype(jnp.float32), kept)
    for r in range(rows):
        keep_ref[r] = jnp.where(source == sta * rows + r, 0.0, kept)
    copies[0].wait()

    def phasors(w, carry):
        usable = valid_ref[win * windows + w].astype(jnp.float32)
        store_phasors(w, phase_ref[w], usable, *own)
        return carry

    lax.fori_loop(0, windows, phasors, 0, unroll=4)


def part_sums(out_ref, block, is_first, groups, weight):
    rows, stations, bins = out_ref.shape
    totals = [jnp.zeros((stations, bins), jnp.float32)] * rows
    for cos_ref, sin_ref, *_ in groups:

        def add(w, totals, cos_ref=cos_ref, sin_ref=sin_ref):
            cosine, sine = cos_ref[w], sin_ref[w]
            added = []
            for r in range(rows):
                row_cos = cos_ref[w, pl.ds(block * rows + r, 1), :]
                row_sin = sin_ref[w, pl.ds(block * rows + r, 1), :]
                left = jnp.where(is_first, row_cos, row_sin)
                right = jnp.where(is_first, row_sin, -row_cos)
                added.append(totals[r] + (left * cosine + right * sine))
            return added

        totals = lax.fori_loop(0, cos_ref.shape[0], add, totals, unroll=6)
    for r in range(rows):
        out_ref[r] = (totals[r] * weight).astype(jnp.bfloat16)


def full_sums(out_ref, block, groups, weight):
    _, rows, stations, bins = out_ref.shape
    totals = [(jnp.zeros((stations, bins), jnp.float32),) * 3] * rows
    for cos_ref, sin_ref, sum_ref, gap_ref in groups:

        def add(w, totals, cos_ref=cos_ref, sin_ref=sin_ref, sum_ref=sum_ref, gap_ref=gap_ref):
            cosine, plus, gap = cos_ref[w], sum_ref[w], gap_ref[w]
            added = []
            for r in range(rows):
                row = pl.ds(block * rows + r, 1)
                both, left, right = totals[r]
                added.append(
                    (
                        both + sum_ref[w, row, :] * cosine,
                        left + sin_ref[w, row, :] * gap,
                        right + cos_ref[w, row, :] * plus,
                    )
                )
            return added

        totals = lax.fori_loop(0, cos_ref.shape[0], add, totals, unroll=6)
    for r in range(rows):
        both, left, right = totals[r]
        out_ref[0, r] = ((both - left) * weight).astype(jnp.bfloat16)
        out_ref[1, r] = ((both - right) * weight).astype(jnp.bfloat16)


def other_kernel(phase_ref, usable_ref, *other):
    def phasors(w, carry):
        store_phasors(w, phase_ref[w], usable_ref[w], *other)
        return carry

    lax.fori_loop(0, phase_ref.shape[0], phasors, 0, unroll=4)


def cross_kernel(rounds, first, phase_ref, usable_ref, weight_ref, *refs):
    own, other, outs = refs[:4], refs[4:8], refs[8:]
    if first:
        other_kernel(phase_ref, usable_ref, *other)
    else:
        outs = outs[1:]
    sta, win = position()
    for (whole, targets), out_ref in zip(rounds, outs):
        block = peer(targets, sta, win == 0)
        if whole:
            full_sums(out_ref, block, (own, other), weight_ref[...])
        else:
            part_sums(out_ref, block, win == 0, (own, other), weight_ref[...])


def table_kernel(blocks, rounds, weight_ref, *refs):
    own, other, (own_part, part_ref, full_ref, row_cos, row_sin) = refs[:4], refs[4:8], refs[8:]
    sta, win = position()
    bins, columns = part_ref.shape[1:]
    wrap = 2 * blocks * bins
    half = columns // 2
    step = 16
    column = lax.broadcasted_iota(jnp.int32, (step, columns), 1)
    is_first = win == 0
    lag = jnp.where(is_first, column - half, jnp.where(column < half, column, column - columns))

    def phasor(index):
        wrapped = ((index + wrap // 2) & (wrap - 1)) - wrap // 2
        return cos_sin(wrapped.astype(jnp.float32) * (2.0 * math.pi / wrap))

    fine = lax.broadcasted_iota(jnp.int32, (step, columns), 0)
    fine_cos, fine_sin = phasor(fine * lag)
    steps = bins // step

    def band_rows(block, store):
        for start in range(0, steps, step):
            coarse = block * bins + (start + fine) * step
            row_cos[...], row_sin[...] = phasor(coarse * lag)

            def fill(a, carry, start=start):
                left_cos = row_cos[pl.ds(a, 1), :]
                left_sin = row_sin[pl.ds(a, 1), :]
                cosine = left_cos * fine_cos - left_sin * fine_sin
                sine = left_sin * fine_cos + left_cos * fine_sin
                store(pl.ds(pl.multiple_of((start + a) * step, step), step), cosine, -sine)
                return carry

            lax.fori_loop(0, min(step, steps - start), fill, 0, unroll=2)

    full = [sources(targets) for whole, targets in rounds if whole]
    (shared,) = [sources(targets) for whole, targets in rounds if not whole]
    for slot, targets in enumerate(full):

        def store_full(place, cosine, sine, slot=slot):
            full_ref[slot, 0, place, :] = cosine.astype(jnp.bfloat16)
            full_ref[slot, 1, place, :] = sine.astype(jnp.bfloat16)

        band_rows(peer(targets, sta, is_first), store_full)
    for slot, block in enumerate((sta, peer(shared, sta, is_first))):

        def store_part(place, cosine, sine, slot=slot):
            part_ref[slot, place, :] = jnp.where(is_first, cosine, sine).astype(jnp.bfloat16)

        band_rows(block, store_part)
    part_sums(own_part, sta, is_first, (own, other), weight_ref[...])


def times(spectra, table):
    pairs = spectra.shape[0] * spectra.shape[1]
    return jnp.dot(spectra.reshape(pairs, -1), table, preferred_element_type=jnp.float32)


def add_slot(total, spectra_ref, slot, part_ref, full_ref, lags):
    if slot < 0:
        return total + times(spectra_ref[...], part_ref[-slot, :, lags])
    for c in range(2):
        total = total + times(spectra_ref[c], full_ref[slot, c, :, lags])
    return total


def early_kernel(slot, before, part_ref, full_ref, before_ref, spectra_ref, out_ref):
    lags = pl.ds(0, out_ref.shape[-1])
    total = before_ref[...] if before else times(before_ref[...], part_ref[0])
    out_ref[...] = add_slot(total, spectra_ref, slot, part_ref, full_ref, lags)


def late_kernel(slots, side, keep_ref, part_ref, full_ref, early_ref, *refs):
    out_ref = refs[-1]
    rows, stations, half = out_ref.shape
    lags = pl.ds(side * half, half)
    total = early_ref[:, lags]
    for slot, spectra_ref in zip(slots, refs[:-1]):
        total = add_slot(total, spectra_ref, slot, part_ref, full_ref, lags)
    out_ref[...] = total.reshape(rows, stations, half) * keep_ref[...]


def per_device(phases, window_valid, freq_taper, pair_mask):
    blocks = lax.axis_size("sta")
    windows, bins, stations = phases.shape
    rows = stations // blocks
    half = LAGS // 2
    rounds = rounds_of(blocks)
    swap = [(0, 1), (1, 0)]

    def kernel(body, name, outs, ins, scratch=()):
        return pl.pallas_call(
            body,
            out_shape=[jax.ShapeDtypeStruct(shape, dtype) for shape, dtype in outs],
            in_specs=ins,
            out_specs=[VMEM] * len(outs),
            scratch_shapes=list(scratch),
            compiler_params=PARAMS,
            name=name,
        )

    f32, bf16 = jnp.float32, jnp.bfloat16
    phasor_set = [((windows, stations, bins), f32)] * 4
    part_shape = ((rows, stations, bins), bf16)
    full_shape = ((2, rows, stations, bins), bf16)
    half_shape = ((rows, stations, half), f32)
    phases = jnp.transpose(phases, (0, 2, 1))
    arriving = lax.ppermute(phases, "win", swap)
    taper = freq_taper
    if bins % 128:
        taper = lax.dynamic_slice_in_dim(freq_taper, lax.axis_index("sta") * bins, bins)
    *own, usable, weight, keep = kernel(
        functools.partial(prepare_kernel, blocks),
        "own_phasors",
        phasor_set + [((windows, 1, bins), f32), ((1, bins), f32), half_shape],
        [ANY] * 4,
        [
            pltpu.VMEM((windows, stations, bins), bf16),
            pltpu.SMEM(window_valid.shape, jnp.int32),
            pltpu.VMEM((1, bins), f32),
            pltpu.SMEM(pair_mask.shape, jnp.int32),
            pltpu.SemaphoreType.DMA((4,)),
        ],
    )(*(in_hbm(array) for array in (phases, window_valid, taper.reshape(1, -1), pair_mask)))
    axes = ("sta", "win")
    sent, shapes = [], {True: full_shape, False: part_shape}
    for first, group in enumerate([[r] for r in rounds] if CHAIN else [rounds]):
        outs = [shapes[whole] for whole, _ in group]
        if not first:
            *other, made = kernel(
                functools.partial(cross_kernel, group, True), "cross_spectra", phasor_set + outs, [VMEM] * 7
            )(arriving, usable, weight, *own)
            sent.append(made)
        else:
            (made,) = kernel(
                functools.partial(cross_kernel, group, False), "cross_spectra", outs, [VMEM] * 12
            )(arriving, usable, weight, *own, *other, sent[-1])
            sent.append(made)
    arrived = []
    for spectra, (_, targets) in zip(sent, rounds):
        moves = [(2 * b + w, 2 * targets[w][b] + w) for b in range(blocks) for w in range(2)]
        arrived.append(lax.ppermute(spectra, axes, moves))
    own_part, part_table, full_table = kernel(
        functools.partial(table_kernel, blocks, rounds),
        "lag_table",
        [part_shape, ((2, bins, LAGS), bf16), ((len(rounds) - 1, 2, bins, LAGS), bf16)],
        [VMEM] * 9,
        [pltpu.VMEM((16, LAGS), f32)] * 2,
    )(weight, *own, *other)
    slots, slot = [], 0
    for whole, _ in rounds:
        slots.append(slot if whole else -1)
        slot += whole
    ahead = len(rounds) - LATE
    early = own_part
    for index in range(ahead):
        (early,) = kernel(
            functools.partial(early_kernel, slots[index], index),
            "lag_sums_early",
            [((rows * stations, LAGS), f32)],
            [VMEM] * 4,
        )(part_table, full_table, early, arrived[index])

    def late(side):
        return kernel(
            functools.partial(late_kernel, slots[ahead:], side),
            "lag_sums_late",
            [half_shape],
            [VMEM] * (4 + LATE),
        )(keep, part_table, full_table, early, *arrived[ahead:])[0]

    theirs = lax.ppermute(late(1), "win", swap)
    return late(0) + theirs


def solution(mesh):
    return jax.shard_map(
        per_device,
        mesh=mesh,
        in_specs=(P(("days", "win"), "sta", None), P("days"), P(), P()),
        out_specs=P(("days", "sta"), None, "win"),
        check_vma=False,
    )
```

```python
import functools
import math

import jax
import jax.numpy as jnp
from jax import lax
from jax.experimental import pallas as pl
from jax.experimental.pallas import tpu as pltpu
from jax.sharding import PartitionSpec as P

LAGS = 512
LATE = 2
BEGUN = 2
ROUNDS = (
    ((3, 5, 1, 7, 2, 6, 0, 4), (5, 7, 4, 6, 1, 2, 3, 0)),
    ((4, 2, 6, 0, 7, 1, 5, 3), (6, 4, 7, 1, 3, 0, 2, 5)),
    ((2, 0, 3, 5, 6, 4, 7, 1), (7, 6, 5, 4, 0, 3, 1, 2)),
    ((1, 3, 0, 2, 5, 7, 4, 6), (1, 3, 0, 2, 5, 7, 4, 6)),
)
VMEM = pl.BlockSpec(memory_space=pltpu.VMEM)
ANY = pl.BlockSpec(memory_space=pl.ANY)
PARAMS = pltpu.CompilerParams(vmem_limit_bytes=48 * 1024 * 1024)

COS_COEF = (
    0.9999999890590218,
    -0.49999989101070386,
    0.041666489217381156,
    -0.001388780359807859,
    2.476988355752502e-05,
    -2.707903082088142e-07,
    1.724509174527214e-09,
)
SIN_COEF = (
    0.9999997571451633,
    -0.06534424613196173,
    0.001711441007161203,
    -2.461450561671638e-05,
    1.977699154629728e-07,
)


def cos_sin(angle):
    square = angle * angle
    cosine = COS_COEF[-1]
    for coef in COS_COEF[-2::-1]:
        cosine = cosine * square + coef
    sine = SIN_COEF[-1]
    for coef in SIN_COEF[-2::-1]:
        sine = sine * square + coef
    sine = sine * (angle - angle * square * (1.0 / math.pi**2))
    return cosine, sine


def rounds_of(blocks):
    rounds = ROUNDS
    if blocks != len(ROUNDS[0][0]):
        steps = [(step, step ^ 1) for step in range(2, blocks, 2)] + [(1, 1)]
        rounds = [tuple(tuple(b ^ step for b in range(blocks)) for step in pair) for pair in steps]
    return [(pair[0] != pair[1], pair) for pair in rounds]


def lookup(values, sta):
    found = jnp.int32(values[0])
    for b, value in enumerate(values[1:], 1):
        found = jnp.where(sta == b, value, found)
    return found


def peer(targets, sta, is_first):
    return jnp.where(is_first, lookup(targets[0], sta), lookup(targets[1], sta))


def sources(targets):
    return tuple(tuple(sorted(range(len(side)), key=lambda b: side[b])) for side in targets)


def in_hbm(array):
    return pltpu.with_memory_space_constraint(array, pltpu.HBM)


def position():
    return lax.axis_index("sta"), lax.axis_index("win")


def store_phasors(w, phase, usable, cos_ref, sin_ref, sum_ref, gap_ref):
    cosine, sine = cos_sin(phase.astype(jnp.float32))
    cosine = cosine.astype(jnp.bfloat16).astype(jnp.float32) * usable
    sine = sine.astype(jnp.bfloat16).astype(jnp.float32) * usable
    cos_ref[w] = cosine
    sin_ref[w] = sine
    sum_ref[w] = cosine + sine
    gap_ref[w] = cosine - sine


def prepare_kernel(blocks, begun, phase_hbm, valid_hbm, taper_hbm, mask_hbm, *refs):
    own, (usable_ref, weight_ref, keep_ref) = refs[:4], refs[4:7]
    begun_refs = refs[7 : 7 + len(begun)]
    phase_ref, valid_ref, taper_ref, mask_ref, sems = refs[7 + len(begun) :]
    sta, win = position()
    windows, stations, bins = phase_ref.shape
    rows = stations // blocks
    if taper_hbm.shape[1] > bins:
        taper_hbm = taper_hbm.at[:, pl.ds(pl.multiple_of(sta * bins, 128), bins)]
    copies = [
        pltpu.make_async_copy(source, target, sems.at[c])
        for c, (source, target) in enumerate(
            (
                (phase_hbm, phase_ref),
                (valid_hbm, valid_ref),
                (taper_hbm, taper_ref),
                (mask_hbm, mask_ref),
            )
        )
    ]
    for copy in copies:
        copy.start()
    for copy in copies[1:]:
        copy.wait()
    count = jnp.float32(0)
    for w in range(2 * windows):
        count += valid_ref[w].astype(jnp.float32)
    total = jnp.maximum(jnp.full((1, bins), count, jnp.float32), 1.0)
    weight_ref[...] = taper_ref[...] * (1.0 / jnp.sqrt(blocks * bins * total))
    for w in range(windows):
        usable = valid_ref[(1 - win) * windows + w].astype(jnp.float32)
        usable_ref[w] = jnp.full((1, bins), usable, jnp.float32)
    source = lax.broadcasted_iota(jnp.int32, keep_ref.shape[1:], 0)
    kept = jnp.zeros(keep_ref.shape[1:], jnp.float32)
    for block in range(blocks):
        kept = jnp.where(source // rows == block, mask_ref[sta, block].astype(jnp.float32), kept)
    for r in range(rows):
        keep_ref[r] = jnp.where(source == sta * rows + r, 0.0, kept)
    copies[0].wait()

    def phasors(w, carry):
        usable = valid_ref[win * windows + w].astype(jnp.float32)
        store_phasors(w, phase_ref[w], usable, *own)
        return carry

    lax.fori_loop(0, windows, phasors, 0, unroll=12)
    for targets, begun_ref in zip(begun, begun_refs):
        block = peer(targets, sta, win == 0)
        totals = add_full(start_full(rows, stations, bins), block, own)
        for r in range(rows):
            for part in range(3):
                begun_ref[r, part] = totals[r][part]


def part_sums(out_ref, block, is_first, groups, weight):
    rows, stations, bins = out_ref.shape
    totals = [jnp.zeros((stations, bins), jnp.float32)] * rows
    for cos_ref, sin_ref, *_ in groups:

        def add(w, totals, cos_ref=cos_ref, sin_ref=sin_ref):
            cosine, sine = cos_ref[w], sin_ref[w]
            added = []
            for r in range(rows):
                row_cos = cos_ref[w, pl.ds(block * rows + r, 1), :]
                row_sin = sin_ref[w, pl.ds(block * rows + r, 1), :]
                left = jnp.where(is_first, row_cos, row_sin)
                right = jnp.where(is_first, row_sin, -row_cos)
                added.append(totals[r] + (left * cosine + right * sine))
            return added

        totals = lax.fori_loop(0, cos_ref.shape[0], add, totals, unroll=6)
    for r in range(rows):
        out_ref[r] = (totals[r] * weight).astype(jnp.bfloat16)


def add_full(totals, block, group):
    cos_ref, sin_ref, sum_ref, gap_ref = group
    rows = len(totals)

    def add(w, totals):
        cosine, plus, gap = cos_ref[w], sum_ref[w], gap_ref[w]
        added = []
        for r in range(rows):
            row = pl.ds(block * rows + r, 1)
            both, left, right = totals[r]
            added.append(
                (
                    both + sum_ref[w, row, :] * cosine,
                    left + sin_ref[w, row, :] * gap,
                    right + cos_ref[w, row, :] * plus,
                )
            )
        return added

    return lax.fori_loop(0, cos_ref.shape[0], add, totals, unroll=6)


def start_full(rows, stations, bins):
    return [(jnp.zeros((stations, bins), jnp.float32),) * 3] * rows


def full_sums(out_ref, block, own, other, weight, begun_ref=None):
    _, rows, stations, bins = out_ref.shape
    if begun_ref is None:
        totals = add_full(start_full(rows, stations, bins), block, own)
    else:
        totals = [tuple(begun_ref[r, part] for part in range(3)) for r in range(rows)]
    totals = add_full(totals, block, other)
    for r in range(rows):
        both, left, right = totals[r]
        out_ref[0, r] = ((both - left) * weight).astype(jnp.bfloat16)
        out_ref[1, r] = ((both - right) * weight).astype(jnp.bfloat16)


def other_kernel(phase_ref, usable_ref, *other):
    def phasors(w, carry):
        store_phasors(w, phase_ref[w], usable_ref[w], *other)
        return carry

    lax.fori_loop(0, phase_ref.shape[0], phasors, 0, unroll=12)


def cross_kernel(round_, first, begun, weight_ref, *refs):
    refs = list(refs)
    own, other = [refs.pop(0) for _ in range(4)], None
    begun_ref = refs.pop(0) if begun else None
    if first:
        phase_ref, usable_ref = refs.pop(0), refs.pop(0)
        other = [refs.pop(0) for _ in range(4)]
        other_kernel(phase_ref, usable_ref, *other)
    else:
        other = [refs.pop(0) for _ in range(4)]
    out_ref = refs[-1]
    sta, win = position()
    whole, targets = round_
    block = peer(targets, sta, win == 0)
    if whole:
        full_sums(out_ref, block, own, other, weight_ref[...], begun_ref)
    else:
        part_sums(out_ref, block, win == 0, (own, other), weight_ref[...])


def table_kernel(blocks, rounds, weight_ref, *refs):
    own, other = refs[:4], refs[4:8]
    own_part, part_ref, full_ref, band_cos, band_sin, row_cos, row_sin = refs[8:]
    sta, win = position()
    bins, columns = part_ref.shape[1:]
    wrap = 2 * blocks * bins
    half = columns // 2
    step = 16
    is_first = win == 0

    def lags(rows):
        column = lax.broadcasted_iota(jnp.int32, (rows, columns), 1)
        return jnp.where(is_first, column - half, jnp.where(column < half, column, column - columns))

    def phasor(index):
        wrapped = ((index + wrap // 2) & (wrap - 1)) - wrap // 2
        return cos_sin(wrapped.astype(jnp.float32) * (2.0 * math.pi / wrap))

    row = lax.broadcasted_iota(jnp.int32, (step, columns), 0)
    fine_cos, fine_sin = phasor(row * lags(step))
    full = [peer(sources(targets), sta, is_first) for whole, targets in rounds if whole]
    part = [sta] + [peer(sources(targets), sta, is_first) for whole, targets in rounds if not whole]
    band = lax.broadcasted_iota(jnp.int32, band_cos.shape, 0)
    first_bin = jnp.zeros(band_cos.shape, jnp.int32)
    for slot, block in enumerate(full + part):
        first_bin = jnp.where(band == slot, block * bins, first_bin)
    band_cos[...], band_sin[...] = phasor(first_bin * lags(band_cos.shape[0]))
    steps = bins // step
    for start in range(0, steps, step):
        coarse_cos, coarse_sin = phasor((start + row) * step * lags(step))
        for slot in range(len(full) + len(part)):
            left_cos, left_sin = band_cos[slot : slot + 1, :], band_sin[slot : slot + 1, :]
            row_cos[...] = left_cos * coarse_cos - left_sin * coarse_sin
            row_sin[...] = -(left_sin * coarse_cos + left_cos * coarse_sin)

            def fill(a, carry, start=start, slot=slot):
                cosine, minus = row_cos[pl.ds(a, 1), :], row_sin[pl.ds(a, 1), :]
                place = pl.ds(pl.multiple_of((start + a) * step, step), step)
                if slot < len(full):
                    value = cosine * fine_cos + minus * fine_sin
                    full_ref[slot, 0, place, :] = value.astype(jnp.bfloat16)
                    value = minus * fine_cos - cosine * fine_sin
                    full_ref[slot, 1, place, :] = value.astype(jnp.bfloat16)
                else:
                    one = jnp.where(is_first, cosine, minus)
                    two = jnp.where(is_first, minus, -cosine)
                    value = one * fine_cos + two * fine_sin
                    part_ref[slot - len(full), place, :] = value.astype(jnp.bfloat16)
                return carry

            lax.fori_loop(0, min(step, steps - start), fill, 0, unroll=4)
    part_sums(own_part, sta, is_first, (own, other), weight_ref[...])


def times(spectra, table):
    pairs = spectra.shape[0] * spectra.shape[1]
    return jnp.dot(spectra.reshape(pairs, -1), table, preferred_element_type=jnp.float32)


def add_slot(total, spectra_ref, slot, part_ref, full_ref, lags):
    if slot < 0:
        return total + times(spectra_ref[...], part_ref[-slot, :, lags])
    for c in range(2):
        total = total + times(spectra_ref[c], full_ref[slot, c, :, lags])
    return total


def early_kernel(slot, before, part_ref, full_ref, before_ref, spectra_ref, out_ref):
    lags = pl.ds(0, out_ref.shape[-1])
    total = before_ref[...] if before else times(before_ref[...], part_ref[0])
    out_ref[...] = add_slot(total, spectra_ref, slot, part_ref, full_ref, lags)


def late_kernel(slots, side, keep_ref, part_ref, full_ref, early_ref, *refs):
    out_ref = refs[-1]
    rows, stations, half = out_ref.shape
    lags = pl.ds(side * half, half)
    total = early_ref[:, lags]
    for slot, spectra_ref in zip(slots, refs[:-1]):
        total = add_slot(total, spectra_ref, slot, part_ref, full_ref, lags)
    out_ref[...] = total.reshape(rows, stations, half) * keep_ref[...]


def final_kernel(mine_ref, theirs_ref, out_hbm, out_ref, sems):
    copies = []
    for r in range(out_ref.shape[0]):
        out_ref[r] = mine_ref[r] + theirs_ref[r]
        copies.append(pltpu.make_async_copy(out_ref.at[r], out_hbm.at[r], sems.at[r]))
        copies[-1].start()
    for copy in copies:
        copy.wait()


def per_device(phases, window_valid, freq_taper, pair_mask):
    blocks = lax.axis_size("sta")
    windows, bins, stations = phases.shape
    rows = stations // blocks
    half = LAGS // 2
    rounds = rounds_of(blocks)
    swap = [(0, 1), (1, 0)]

    def kernel(body, name, outs, ins, scratch=()):
        return pl.pallas_call(
            body,
            out_shape=[jax.ShapeDtypeStruct(shape, dtype) for shape, dtype in outs],
            in_specs=ins,
            out_specs=[VMEM] * len(outs),
            scratch_shapes=list(scratch),
            compiler_params=PARAMS,
            name=name,
        )

    f32, bf16 = jnp.float32, jnp.bfloat16
    phasor_set = [((windows, stations, bins), f32)] * 4
    part_shape = ((rows, stations, bins), bf16)
    full_shape = ((2, rows, stations, bins), bf16)
    half_shape = ((rows, stations, half), f32)
    phases = jnp.transpose(phases, (0, 2, 1))
    arriving = lax.ppermute(phases, "win", swap)
    taper = freq_taper
    if bins % 128:
        taper = lax.dynamic_slice_in_dim(freq_taper, lax.axis_index("sta") * bins, bins)
    begun = [targets for whole, targets in rounds[:BEGUN] if whole]
    made = kernel(
        functools.partial(prepare_kernel, blocks, begun),
        "own_phasors",
        phasor_set
        + [((windows, 1, bins), f32), ((1, bins), f32), half_shape]
        + [((rows, 3, stations, bins), f32)] * len(begun),
        [ANY] * 4,
        [
            pltpu.VMEM((windows, stations, bins), bf16),
            pltpu.SMEM(window_valid.shape, jnp.int32),
            pltpu.VMEM((1, bins), f32),
            pltpu.SMEM(pair_mask.shape, jnp.int32),
            pltpu.SemaphoreType.DMA((4,)),
        ],
    )(*(in_hbm(array) for array in (phases, window_valid, taper.reshape(1, -1), pair_mask)))
    own, (usable, weight, keep), started = made[:4], made[4:7], list(made[7:])
    axes = ("sta", "win")
    sent, other = [], None
    for index, round_ in enumerate(rounds):
        early = round_[0] and index < BEGUN
        args = [weight, *own] + ([started.pop(0)] if early else [])
        outs = [full_shape if round_[0] else part_shape]
        if not index:
            args += [arriving, usable]
            outs = phasor_set + outs
        else:
            args += [*other, sent[-1]]
        *made, payload = kernel(
            functools.partial(cross_kernel, round_, not index, early),
            "cross_spectra",
            outs,
            [VMEM] * len(args),
        )(*args)
        other = other or made
        sent.append(payload)
    arrived = []
    for spectra, (_, targets) in zip(sent, rounds):
        moves = [(2 * b + w, 2 * targets[w][b] + w) for b in range(blocks) for w in range(2)]
        arrived.append(lax.ppermute(spectra, axes, moves))
    own_part, part_table, full_table = kernel(
        functools.partial(table_kernel, blocks, rounds),
        "lag_table",
        [part_shape, ((2, bins, LAGS), bf16), ((len(rounds) - 1, 2, bins, LAGS), bf16)],
        [VMEM] * 9,
        [pltpu.VMEM((-(-(len(rounds) + 1) // 8) * 8, LAGS), f32)] * 2
        + [pltpu.VMEM((16, LAGS), f32)] * 2,
    )(weight, *own, *other)
    slots, slot = [], 0
    for whole, _ in rounds:
        slots.append(slot if whole else -1)
        slot += whole
    ahead = len(rounds) - LATE
    early = own_part
    for index in range(ahead):
        (early,) = kernel(
            functools.partial(early_kernel, slots[index], index),
            "lag_sums_early",
            [((rows * stations, LAGS), f32)],
            [VMEM] * 4,
        )(part_table, full_table, early, arrived[index])

    def late(side):
        return kernel(
            functools.partial(late_kernel, slots[ahead:], side),
            "lag_sums_late",
            [half_shape],
            [VMEM] * (4 + LATE),
        )(keep, part_table, full_table, early, *arrived[ahead:])[0]

    theirs = lax.ppermute(late(1), "win", swap)
    return pl.pallas_call(
        final_kernel,
        out_shape=jax.ShapeDtypeStruct(*half_shape),
        in_specs=[VMEM] * 2,
        out_specs=ANY,
        scratch_shapes=[pltpu.VMEM(*half_shape), pltpu.SemaphoreType.DMA((rows,))],
        compiler_params=PARAMS,
        name="correlations",
    )(late(0), theirs)


def solution(mesh):
    return jax.shard_map(
        per_device,
        mesh=mesh,
        in_specs=(P(("days", "win"), "sta", None), P("days"), P(), P()),
        out_specs=P(("days", "sta"), None, "win"),
        check_vma=False,
    )
```

```python
import functools
import math

import jax
import jax.numpy as jnp
from jax import lax
from jax.experimental import pallas as pl
from jax.experimental.pallas import tpu as pltpu
from jax.sharding import PartitionSpec as P

LAGS = 512
BEGUN = 2
SMALL = 1000
ROUNDS = (
    ((3, 2, 6, 7, 5, 1, 0, 4), (4, 7, 1, 5, 3, 6, 2, 0)),
    ((6, 5, 7, 4, 0, 2, 1, 3), (7, 4, 5, 6, 1, 0, 3, 2)),
    ((1, 0, 4, 2, 7, 3, 5, 6), (5, 6, 3, 0, 2, 7, 4, 1)),
    ((2, 3, 0, 1, 6, 4, 7, 5), (2, 3, 0, 1, 6, 4, 7, 5)),
)
VMEM = pl.BlockSpec(memory_space=pltpu.VMEM)
ANY = pl.BlockSpec(memory_space=pl.ANY)
PARAMS = pltpu.CompilerParams(vmem_limit_bytes=48 * 1024 * 1024)

COS_COEF = (
    0.9999999890590218,
    -0.49999989101070386,
    0.041666489217381156,
    -0.001388780359807859,
    2.476988355752502e-05,
    -2.707903082088142e-07,
    1.724509174527214e-09,
)
SIN_COEF = (
    0.9999997571451633,
    -0.06534424613196173,
    0.001711441007161203,
    -2.461450561671638e-05,
    1.977699154629728e-07,
)


def cos_sin(angle):
    square = angle * angle
    cosine = COS_COEF[-1]
    for coef in COS_COEF[-2::-1]:
        cosine = cosine * square + coef
    sine = SIN_COEF[-1]
    for coef in SIN_COEF[-2::-1]:
        sine = sine * square + coef
    sine = sine * (angle - angle * square * (1.0 / math.pi**2))
    return cosine, sine


def rounds_of(blocks):
    if blocks == len(ROUNDS[0][0]):
        return ROUNDS
    steps = [(step, step ^ 1) for step in range(2, blocks, 2)] + [(1, 1)]
    return tuple(tuple(tuple(b ^ step for b in range(blocks)) for step in pair) for pair in steps)


def lookup(values, sta):
    found = jnp.int32(values[0])
    for b, value in enumerate(values[1:], 1):
        found = jnp.where(sta == b, value, found)
    return found


def peer(targets, sta, is_first):
    return jnp.where(is_first, lookup(targets[0], sta), lookup(targets[1], sta))


def sources(targets):
    return tuple(tuple(sorted(range(len(side)), key=lambda b: side[b])) for side in targets)


def in_hbm(array):
    return pltpu.with_memory_space_constraint(array, pltpu.HBM)


def position():
    return lax.axis_index("sta"), lax.axis_index("win")


def store_phasors(w, phase, usable, cos_ref, sin_ref, sum_ref, gap_ref):
    cosine, sine = cos_sin(phase.astype(jnp.float32))
    cosine = cosine.astype(jnp.bfloat16).astype(jnp.float32) * usable
    sine = sine.astype(jnp.bfloat16).astype(jnp.float32) * usable
    cos_ref[w] = cosine
    sin_ref[w] = sine
    sum_ref[w] = cosine + sine
    gap_ref[w] = cosine - sine


def prepare_kernel(blocks, begun, phase_hbm, valid_hbm, taper_hbm, mask_hbm, *refs):
    own, (usable_ref, weight_ref, keep_ref) = refs[:4], refs[4:7]
    begun_refs = refs[7 : 7 + len(begun)]
    phase_ref, valid_ref, taper_ref, mask_ref, sems = refs[7 + len(begun) :]
    sta, win = position()
    windows, stations, bins = phase_ref.shape
    rows = stations // blocks
    if taper_hbm.shape[1] > bins:
        taper_hbm = taper_hbm.at[:, pl.ds(pl.multiple_of(sta * bins, 128), bins)]
    copies = [
        pltpu.make_async_copy(source, target, sems.at[c])
        for c, (source, target) in enumerate(
            (
                (phase_hbm, phase_ref),
                (valid_hbm, valid_ref),
                (taper_hbm, taper_ref),
                (mask_hbm, mask_ref),
            )
        )
    ]
    for copy in copies:
        copy.start()
    for copy in copies[1:]:
        copy.wait()
    count = jnp.float32(0)
    for w in range(2 * windows):
        count += valid_ref[w].astype(jnp.float32)
    total = jnp.maximum(jnp.full((1, bins), count, jnp.float32), 1.0)
    weight_ref[...] = taper_ref[...] * (1.0 / jnp.sqrt(blocks * bins * total))
    for w in range(windows):
        usable = valid_ref[(1 - win) * windows + w].astype(jnp.float32)
        usable_ref[w] = jnp.full((1, bins), usable, jnp.float32)
    source = lax.broadcasted_iota(jnp.int32, keep_ref.shape[1:], 0)
    kept = jnp.zeros(keep_ref.shape[1:], jnp.float32)
    for block in range(blocks):
        kept = jnp.where(source // rows == block, mask_ref[sta, block].astype(jnp.float32), kept)
    for r in range(rows):
        keep_ref[r] = jnp.where(source == sta * rows + r, 0.0, kept)
    copies[0].wait()

    def phasors(w, carry):
        usable = valid_ref[win * windows + w].astype(jnp.float32)
        store_phasors(w, phase_ref[w], usable, *own)
        return carry

    lax.fori_loop(0, windows, phasors, 0, unroll=4)
    for targets, begun_ref in zip(begun, begun_refs):
        block = peer(targets, sta, win == 0)
        totals = add_full(start_full(rows, stations, bins), block, own)
        for r in range(rows):
            for part in range(3):
                begun_ref[r, part] = totals[r][part]


def add_full(totals, block, group):
    cos_ref, sin_ref, sum_ref, gap_ref = group
    rows = len(totals)

    def add(w, totals):
        cosine, plus, gap = cos_ref[w], sum_ref[w], gap_ref[w]
        added = []
        for r in range(rows):
            row = pl.ds(block * rows + r, 1)
            both, left, right = totals[r]
            added.append(
                (
                    both + sum_ref[w, row, :] * cosine,
                    left + sin_ref[w, row, :] * gap,
                    right + cos_ref[w, row, :] * plus,
                )
            )
        return added

    return lax.fori_loop(0, cos_ref.shape[0], add, totals, unroll=6)


def start_full(rows, stations, bins):
    return [(jnp.zeros((stations, bins), jnp.float32),) * 3] * rows


def full_sums(out_ref, block, own, other, weight, begun_ref=None):
    _, rows, stations, bins = out_ref.shape
    if begun_ref is None:
        totals = add_full(start_full(rows, stations, bins), block, own)
    else:
        totals = [tuple(begun_ref[r, part] for part in range(3)) for r in range(rows)]
    totals = add_full(totals, block, other)
    for r in range(rows):
        both, left, right = totals[r]
        out_ref[0, r] = ((both - left) * weight).astype(jnp.bfloat16).astype(out_ref.dtype)
        out_ref[1, r] = ((both - right) * weight).astype(jnp.bfloat16).astype(out_ref.dtype)


def other_kernel(phase_ref, usable_ref, *other):
    def phasors(w, carry):
        store_phasors(w, phase_ref[w], usable_ref[w], *other)
        return carry

    lax.fori_loop(0, phase_ref.shape[0], phasors, 0, unroll=12)


def cross_kernel(targets, first, begun, weight_ref, *refs):
    refs = list(refs)
    own, other = [refs.pop(0) for _ in range(4)], None
    begun_ref = refs.pop(0) if begun else None
    if first:
        phase_ref, usable_ref = refs.pop(0), refs.pop(0)
        other = [refs.pop(0) for _ in range(4)]
        other_kernel(phase_ref, usable_ref, *other)
    else:
        other = [refs.pop(0) for _ in range(4)]
    out_ref = refs[-1]
    sta, win = position()
    block = peer(targets, sta, win == 0)
    full_sums(out_ref, block, own, other, weight_ref[...], begun_ref)


def fill_tables(blocks, bands, table_ref, band_cos, band_sin, row_cos, row_sin):
    _, win = position()
    bins, columns = table_ref.shape[2:]
    wrap = 2 * blocks * bins
    half = LAGS // 2
    step = 16
    is_first = win == 0

    def lags(rows):
        column = lax.broadcasted_iota(jnp.int32, (rows, columns), 1)
        return jnp.where(is_first, column - half, jnp.where(column < half, column, column - LAGS))

    def phasor(index):
        wrapped = ((index + wrap // 2) & (wrap - 1)) - wrap // 2
        return cos_sin(wrapped.astype(jnp.float32) * (2.0 * math.pi / wrap))

    row = lax.broadcasted_iota(jnp.int32, (step, columns), 0)
    fine_cos, fine_sin = phasor(row * lags(step))
    band = lax.broadcasted_iota(jnp.int32, band_cos.shape, 0)
    first_bin = jnp.zeros(band_cos.shape, jnp.int32)
    for slot, block in enumerate(bands):
        first_bin = jnp.where(band == slot, block * bins, first_bin)
    band_cos[...], band_sin[...] = phasor(first_bin * lags(band_cos.shape[0]))
    steps = bins // step
    for start in range(0, steps, step):
        coarse_cos, coarse_sin = phasor((start + row) * step * lags(step))
        for slot in range(len(bands)):
            left_cos, left_sin = band_cos[slot : slot + 1, :], band_sin[slot : slot + 1, :]
            row_cos[...] = left_cos * coarse_cos - left_sin * coarse_sin
            row_sin[...] = -(left_sin * coarse_cos + left_cos * coarse_sin)

            def fill(a, carry, start=start, slot=slot):
                cosine, minus = row_cos[pl.ds(a, 1), :], row_sin[pl.ds(a, 1), :]
                place = pl.ds(pl.multiple_of((start + a) * step, step), step)
                value = cosine * fine_cos + minus * fine_sin
                table_ref[slot, 0, place, :] = value.astype(jnp.bfloat16)
                value = minus * fine_cos - cosine * fine_sin
                table_ref[slot, 1, place, :] = value.astype(jnp.bfloat16)
                return carry

            lax.fori_loop(0, min(step, steps - start), fill, 0, unroll=4)


def split_table_kernel(blocks, rounds, after_ref, table_ref, *scratch):
    sta, win = position()
    bands = [peer(sources(targets), sta, win == 0) for targets in rounds[:-1]]
    fill_tables(blocks, bands, table_ref, *scratch)


def whole_table_kernel(blocks, rounds, weight_ref, *refs):
    own, other, (after_ref, own_ref, table_ref, *scratch) = refs[:4], refs[4:8], refs[8:]
    sta, win = position()
    bands = [peer(sources(rounds[-1]), sta, win == 0), sta]
    fill_tables(blocks, bands, table_ref, *scratch)
    full_sums(own_ref, sta, own, other, weight_ref[...])


def times(spectra_ref, table_ref):
    _, rows, stations, bins = spectra_ref.shape
    total = 0.0
    for c in range(2):
        spectra = spectra_ref[c].reshape(rows * stations, bins).astype(jnp.bfloat16)
        total = total + jnp.dot(spectra, table_ref[c], preferred_element_type=jnp.float32)
    return total


def split_kernel(slot, end, table_ref, *refs):
    outs = 2 if end else 1
    spectra_ref, *before = refs[:-outs]
    total = times(spectra_ref, table_ref.at[slot])
    for before_ref in before:
        total = total + before_ref[...]
    if end:
        mine_ref, theirs_ref = refs[-2:]
        half = mine_ref.shape[-1]
        mine_ref[...], theirs_ref[...] = total[:, :half], total[:, half:].astype(theirs_ref.dtype)
    else:
        refs[-1][...] = total


def whole_kernel(slot, table_ref, spectra_ref, before_ref, out_ref):
    out_ref[...] = before_ref[...] + times(spectra_ref, table_ref.at[slot])


def final_kernel(keep_ref, mine_ref, theirs_ref, out_hbm, out_ref, sems):
    rows, stations, half = out_ref.shape
    copies = []
    for r in range(rows):
        row = pl.ds(r * stations, stations)
        out_ref[r] = (mine_ref[row] + theirs_ref[row].astype(jnp.float32)) * keep_ref[r]
        copies.append(pltpu.make_async_copy(out_ref.at[r], out_hbm.at[r], sems.at[r]))
        copies[-1].start()
    for copy in copies:
        copy.wait()


def per_device(phases, window_valid, freq_taper, pair_mask):
    blocks = lax.axis_size("sta")
    windows, bins, stations = phases.shape
    rows = stations // blocks
    half = LAGS // 2
    rounds = rounds_of(blocks)
    swap = [(0, 1), (1, 0)]

    def kernel(body, name, outs, ins, scratch=(), flops=None):
        return pl.pallas_call(
            body,
            out_shape=[jax.ShapeDtypeStruct(shape, dtype) for shape, dtype in outs],
            in_specs=ins,
            out_specs=[VMEM] * len(outs),
            scratch_shapes=list(scratch),
            compiler_params=PARAMS,
            cost_estimate=flops and pl.CostEstimate(flops=flops, bytes_accessed=1000, transcendentals=0),
            name=name,
        )

    f32, bf16 = jnp.float32, jnp.bfloat16
    phasor_set = [((windows, stations, bins), f32)] * 4
    full_shape = ((2, rows, stations, bins), bf16)
    half_shape = ((rows, stations, half), f32)
    phases = jnp.transpose(phases, (0, 2, 1))
    arriving = lax.ppermute(phases, "win", swap)
    taper = freq_taper
    if bins % 128:
        taper = lax.dynamic_slice_in_dim(freq_taper, lax.axis_index("sta") * bins, bins)
    begun = rounds[:BEGUN]
    made = kernel(
        functools.partial(prepare_kernel, blocks, begun),
        "own_phasors",
        phasor_set
        + [((windows, 1, bins), f32), ((1, bins), f32), half_shape]
        + [((rows, 3, stations, bins), f32)] * len(begun),
        [ANY] * 4,
        [
            pltpu.VMEM((windows, stations, bins), bf16),
            pltpu.SMEM(window_valid.shape, jnp.int32),
            pltpu.VMEM((1, bins), f32),
            pltpu.SMEM(pair_mask.shape, jnp.int32),
            pltpu.SemaphoreType.DMA((4,)),
        ],
    )(*(in_hbm(array) for array in (phases, window_valid, taper.reshape(1, -1), pair_mask)))
    own, (usable, weight, keep), started = made[:4], made[4:7], made[7:]
    axes = ("sta", "win")
    sent, other = [], None
    for index, targets in enumerate(rounds):
        args = [weight, *own, *started[index : index + 1]]
        args += [*other, sent[-1]] if index else [arriving, usable]
        *made, payload = kernel(
            functools.partial(cross_kernel, targets, not index, index < len(begun)),
            "cross_spectra",
            ([] if index else phasor_set) + [full_shape],
            [VMEM] * len(args),
        )(*args)
        other = other or made
        sent.append(payload)
    arrived = []
    for spectra, targets in zip(sent, rounds):
        moves = [(2 * b + w, 2 * targets[w][b] + w) for b in range(blocks) for w in range(2)]
        arrived.append(lax.ppermute(spectra, axes, moves))
    split = len(rounds) - 1
    def scratch(slots, lags):
        return [pltpu.VMEM((-(-slots // 8) * 8, lags), f32)] * 2 + [pltpu.VMEM((16, lags), f32)] * 2

    (split_table,) = kernel(
        functools.partial(split_table_kernel, blocks, rounds),
        "split_lag_table",
        [((split, 2, bins, LAGS), bf16)],
        [VMEM],
        scratch(split, LAGS),
    )(sent[-1])
    pairs, sums = rows * stations, []
    for slot in range(split):
        end = slot == split - 1
        sums = kernel(
            functools.partial(split_kernel, slot, end),
            "split_lag_sums",
            [((pairs, half), f32)] * 2 if end else [((pairs, LAGS), f32)],
            [VMEM] * (2 + len(sums)),
            flops=SMALL,
        )(split_table, arrived[slot], *sums)
    mine, theirs = sums
    theirs = lax.ppermute(theirs, "win", swap)
    own_spectra, whole_table = kernel(
        functools.partial(whole_table_kernel, blocks, rounds),
        "whole_lag_table",
        [full_shape, ((2, 2, bins, half), bf16)],
        [VMEM] * 10,
        scratch(2, half),
    )(weight, *own, *other, mine)
    for slot, spectra in ((1, own_spectra), (0, arrived[-1])):
        (mine,) = kernel(
            functools.partial(whole_kernel, slot),
            "whole_lag_sums",
            [((pairs, half), f32)],
            [VMEM] * 3,
            flops=SMALL,
        )(whole_table, spectra, mine)
    return pl.pallas_call(
        final_kernel,
        out_shape=jax.ShapeDtypeStruct(*half_shape),
        in_specs=[VMEM] * 3,
        out_specs=ANY,
        scratch_shapes=[pltpu.VMEM(*half_shape), pltpu.SemaphoreType.DMA((rows,))],
        compiler_params=PARAMS,
        name="correlations",
    )(keep, mine, theirs)


def solution(mesh):
    return jax.shard_map(
        per_device,
        mesh=mesh,
        in_specs=(P(("days", "win"), "sta", None), P("days"), P(), P()),
        out_specs=P(("days", "sta"), None, "win"),
        check_vma=False,
    )
```

```python
import functools
import math

import jax
import jax.numpy as jnp
from jax import lax
from jax.experimental import pallas as pl
from jax.experimental.pallas import tpu as pltpu
from jax.sharding import PartitionSpec as P

LAGS = 512
BEGUN = 2
SMALL = 1000
ROUNDS = (
    ((2, 3, 6, 5, 1, 7, 4, 0), (4, 6, 5, 0, 7, 3, 1, 2)),
    ((6, 4, 7, 1, 2, 0, 3, 5), (5, 7, 1, 4, 6, 2, 0, 3)),
    ((3, 0, 4, 2, 5, 1, 7, 6), (7, 5, 3, 6, 0, 4, 2, 1)),
    ((1, 2, 0, 7, 3, 6, 5, 4), (1, 2, 0, 7, 3, 6, 5, 4)),
)
VMEM = pl.BlockSpec(memory_space=pltpu.VMEM)
ANY = pl.BlockSpec(memory_space=pl.ANY)
PARAMS = pltpu.CompilerParams(vmem_limit_bytes=48 * 1024 * 1024)

COS_COEF = (
    0.9999999890590218,
    -0.49999989101070386,
    0.041666489217381156,
    -0.001388780359807859,
    2.476988355752502e-05,
    -2.707903082088142e-07,
    1.724509174527214e-09,
)
SIN_COEF = (
    0.9999997571451633,
    -0.06534424613196173,
    0.001711441007161203,
    -2.461450561671638e-05,
    1.977699154629728e-07,
)


def cos_sin(angle):
    square = angle * angle
    cosine = COS_COEF[-1]
    for coef in COS_COEF[-2::-1]:
        cosine = cosine * square + coef
    sine = SIN_COEF[-1]
    for coef in SIN_COEF[-2::-1]:
        sine = sine * square + coef
    sine = sine * (angle - angle * square * (1.0 / math.pi**2))
    return cosine, sine


def rounds_of(blocks):
    if blocks == len(ROUNDS[0][0]):
        return ROUNDS
    steps = [(step, step ^ 1) for step in range(2, blocks, 2)] + [(1, 1)]
    return tuple(tuple(tuple(b ^ step for b in range(blocks)) for step in pair) for pair in steps)


def lookup(values, sta):
    found = jnp.int32(values[0])
    for b, value in enumerate(values[1:], 1):
        found = jnp.where(sta == b, value, found)
    return found


def peer(targets, sta, is_first):
    return jnp.where(is_first, lookup(targets[0], sta), lookup(targets[1], sta))


def sources(targets):
    return tuple(tuple(sorted(range(len(side)), key=lambda b: side[b])) for side in targets)


def in_hbm(array):
    return pltpu.with_memory_space_constraint(array, pltpu.HBM)


def position():
    return lax.axis_index("sta"), lax.axis_index("win")


def store_phasors(w, phase, usable, cos_ref, sin_ref, sum_ref, gap_ref):
    cosine, sine = cos_sin(phase.astype(jnp.float32))
    cosine = cosine.astype(jnp.bfloat16).astype(jnp.float32) * usable
    sine = sine.astype(jnp.bfloat16).astype(jnp.float32) * usable
    cos_ref[w] = cosine
    sin_ref[w] = sine
    sum_ref[w] = cosine + sine
    gap_ref[w] = cosine - sine


def prepare_kernel(blocks, begun, phase_hbm, valid_hbm, taper_hbm, mask_hbm, *refs):
    own, (usable_ref, weight_ref, keep_ref) = refs[:4], refs[4:7]
    begun_refs = refs[7 : 7 + len(begun)]
    phase_ref, valid_ref, taper_ref, mask_ref, sems = refs[7 + len(begun) :]
    sta, win = position()
    windows, stations, bins = phase_ref.shape
    rows = stations // blocks
    if taper_hbm.shape[1] > bins:
        taper_hbm = taper_hbm.at[:, pl.ds(pl.multiple_of(sta * bins, 128), bins)]
    copies = [
        pltpu.make_async_copy(source, target, sems.at[c])
        for c, (source, target) in enumerate(
            (
                (phase_hbm, phase_ref),
                (valid_hbm, valid_ref),
                (taper_hbm, taper_ref),
                (mask_hbm, mask_ref),
            )
        )
    ]
    for copy in copies:
        copy.start()
    for copy in copies[1:]:
        copy.wait()
    count = jnp.float32(0)
    for w in range(2 * windows):
        count += valid_ref[w].astype(jnp.float32)
    total = jnp.maximum(jnp.full((1, bins), count, jnp.float32), 1.0)
    weight_ref[...] = taper_ref[...] * (1.0 / jnp.sqrt(blocks * bins * total))
    for w in range(windows):
        usable = valid_ref[(1 - win) * windows + w].astype(jnp.float32)
        usable_ref[w] = jnp.full((1, bins), usable, jnp.float32)
    source = lax.broadcasted_iota(jnp.int32, keep_ref.shape[1:], 0)
    kept = jnp.zeros(keep_ref.shape[1:], jnp.float32)
    for block in range(blocks):
        kept = jnp.where(source // rows == block, mask_ref[sta, block].astype(jnp.float32), kept)
    for r in range(rows):
        keep_ref[r] = jnp.where(source == sta * rows + r, 0.0, kept)
    copies[0].wait()

    def phasors(w, carry):
        usable = valid_ref[win * windows + w].astype(jnp.float32)
        store_phasors(w, phase_ref[w], usable, *own)
        return carry

    lax.fori_loop(0, windows, phasors, 0, unroll=4)
    for targets, begun_ref in zip(begun, begun_refs):
        block = peer(targets, sta, win == 0)
        totals = add_full(start_full(rows, stations, bins), block, own)
        for r in range(rows):
            for part in range(3):
                begun_ref[r, part] = totals[r][part]


def add_full(totals, block, group):
    cos_ref, sin_ref, sum_ref, gap_ref = group
    rows = len(totals)

    def add(w, totals):
        cosine, plus, gap = cos_ref[w], sum_ref[w], gap_ref[w]
        added = []
        for r in range(rows):
            row = pl.ds(block * rows + r, 1)
            both, left, right = totals[r]
            added.append(
                (
                    both + sum_ref[w, row, :] * cosine,
                    left + sin_ref[w, row, :] * gap,
                    right + cos_ref[w, row, :] * plus,
                )
            )
        return added

    return lax.fori_loop(0, cos_ref.shape[0], add, totals, unroll=6)


def start_full(rows, stations, bins):
    return [(jnp.zeros((stations, bins), jnp.float32),) * 3] * rows


def full_sums(out_ref, block, own, other, weight, begun_ref=None):
    _, rows, stations, bins = out_ref.shape
    if begun_ref is None:
        totals = add_full(start_full(rows, stations, bins), block, own)
    else:
        totals = [tuple(begun_ref[r, part] for part in range(3)) for r in range(rows)]
    totals = add_full(totals, block, other)
    for r in range(rows):
        both, left, right = totals[r]
        out_ref[0, r] = ((both - left) * weight).astype(jnp.bfloat16).astype(out_ref.dtype)
        out_ref[1, r] = ((both - right) * weight).astype(jnp.bfloat16).astype(out_ref.dtype)


def other_kernel(phase_ref, usable_ref, *other):
    def phasors(w, carry):
        store_phasors(w, phase_ref[w], usable_ref[w], *other)
        return carry

    lax.fori_loop(0, phase_ref.shape[0], phasors, 0, unroll=12)


def cross_kernel(targets, first, begun, weight_ref, *refs):
    refs = list(refs)
    own, other = [refs.pop(0) for _ in range(4)], None
    begun_ref = refs.pop(0) if begun else None
    if first:
        phase_ref, usable_ref = refs.pop(0), refs.pop(0)
        other = [refs.pop(0) for _ in range(4)]
        other_kernel(phase_ref, usable_ref, *other)
    else:
        other = [refs.pop(0) for _ in range(4)]
    out_ref = refs[-1]
    sta, win = position()
    block = peer(targets, sta, win == 0)
    full_sums(out_ref, block, own, other, weight_ref[...], begun_ref)


def fill_tables(blocks, bands, table_ref, band_cos, band_sin, row_cos, row_sin):
    _, win = position()
    bins, columns = table_ref.shape[2:]
    wrap = 2 * blocks * bins
    half = LAGS // 2
    step = 16
    is_first = win == 0

    def lags(rows):
        column = lax.broadcasted_iota(jnp.int32, (rows, columns), 1)
        return jnp.where(is_first, column - half, jnp.where(column < half, column, column - LAGS))

    def phasor(index):
        wrapped = ((index + wrap // 2) & (wrap - 1)) - wrap // 2
        return cos_sin(wrapped.astype(jnp.float32) * (2.0 * math.pi / wrap))

    row = lax.broadcasted_iota(jnp.int32, (step, columns), 0)
    fine_cos, fine_sin = phasor(row * lags(step))
    band = lax.broadcasted_iota(jnp.int32, band_cos.shape, 0)
    first_bin = jnp.zeros(band_cos.shape, jnp.int32)
    for slot, block in enumerate(bands):
        first_bin = jnp.where(band == slot, block * bins, first_bin)
    band_cos[...], band_sin[...] = phasor(first_bin * lags(band_cos.shape[0]))
    steps = bins // step
    for start in range(0, steps, step):
        coarse_cos, coarse_sin = phasor((start + row) * step * lags(step))
        for slot in range(len(bands)):
            left_cos, left_sin = band_cos[slot : slot + 1, :], band_sin[slot : slot + 1, :]
            row_cos[...] = left_cos * coarse_cos - left_sin * coarse_sin
            row_sin[...] = -(left_sin * coarse_cos + left_cos * coarse_sin)

            def fill(a, carry, start=start, slot=slot):
                cosine, minus = row_cos[pl.ds(a, 1), :], row_sin[pl.ds(a, 1), :]
                place = pl.ds(pl.multiple_of((start + a) * step, step), step)
                value = cosine * fine_cos + minus * fine_sin
                table_ref[slot, 0, place, :] = value.astype(jnp.bfloat16)
                value = minus * fine_cos - cosine * fine_sin
                table_ref[slot, 1, place, :] = value.astype(jnp.bfloat16)
                return carry

            lax.fori_loop(0, min(step, steps - start), fill, 0, unroll=4)


def split_table_kernel(blocks, rounds, after_ref, table_ref, *scratch):
    sta, win = position()
    bands = [peer(sources(targets), sta, win == 0) for targets in rounds[:-1]]
    fill_tables(blocks, bands, table_ref, *scratch)


def whole_table_kernel(blocks, rounds, weight_ref, *refs):
    own, other, (after_ref, own_ref, table_ref, *scratch) = refs[:4], refs[4:8], refs[8:]
    sta, win = position()
    bands = [peer(sources(rounds[-1]), sta, win == 0), sta]
    fill_tables(blocks, bands, table_ref, *scratch)
    full_sums(own_ref, sta, own, other, weight_ref[...])


def times(spectra_ref, table_ref, slot, lags):
    _, rows, stations, bins = spectra_ref.shape
    total = 0.0
    for c in range(2):
        spectra = spectra_ref[c].reshape(rows * stations, bins)
        table = table_ref[slot, c, :, lags]
        total = total + jnp.dot(spectra, table, preferred_element_type=jnp.float32)
    return total


def sums_kernel(slot, first_lag, table_ref, spectra_ref, *refs):
    *before, out_ref = refs
    lags = pl.ds(first_lag, out_ref.shape[-1])
    total = times(spectra_ref, table_ref, slot, lags)
    for before_ref in before:
        total = total + before_ref[:, lags]
    out_ref[...] = total


def mine_kernel(slot, split_ref, whole_ref, spectra_ref, own_ref, before_ref, out_ref):
    lags = pl.ds(0, out_ref.shape[-1])
    total = before_ref[:, lags] + times(spectra_ref, split_ref, slot, lags)
    out_ref[...] = total + times(own_ref, whole_ref, 1, lags)


def per_device(phases, window_valid, freq_taper, pair_mask):
    blocks = lax.axis_size("sta")
    windows, bins, stations = phases.shape
    rows = stations // blocks
    half = LAGS // 2
    rounds = rounds_of(blocks)
    swap = [(0, 1), (1, 0)]

    def kernel(body, name, outs, ins, scratch=(), flops=None):
        return pl.pallas_call(
            body,
            out_shape=[jax.ShapeDtypeStruct(shape, dtype) for shape, dtype in outs],
            in_specs=ins,
            out_specs=[VMEM] * len(outs),
            scratch_shapes=list(scratch),
            compiler_params=PARAMS,
            cost_estimate=flops and pl.CostEstimate(flops=flops, bytes_accessed=1000, transcendentals=0),
            name=name,
        )

    f32, bf16 = jnp.float32, jnp.bfloat16
    phasor_set = [((windows, stations, bins), f32)] * 4
    full_shape = ((2, rows, stations, bins), bf16)
    half_shape = ((rows, stations, half), f32)
    phases = jnp.transpose(phases, (0, 2, 1))
    arriving = lax.ppermute(phases, "win", swap)
    taper = freq_taper
    if bins % 128:
        taper = lax.dynamic_slice_in_dim(freq_taper, lax.axis_index("sta") * bins, bins)
    begun = rounds[:BEGUN]
    made = kernel(
        functools.partial(prepare_kernel, blocks, begun),
        "own_phasors",
        phasor_set
        + [((windows, 1, bins), f32), ((1, bins), f32), half_shape]
        + [((rows, 3, stations, bins), f32)] * len(begun),
        [ANY] * 4,
        [
            pltpu.VMEM((windows, stations, bins), bf16),
            pltpu.SMEM(window_valid.shape, jnp.int32),
            pltpu.VMEM((1, bins), f32),
            pltpu.SMEM(pair_mask.shape, jnp.int32),
            pltpu.SemaphoreType.DMA((4,)),
        ],
    )(*(in_hbm(array) for array in (phases, window_valid, taper.reshape(1, -1), pair_mask)))
    own, (usable, weight, keep), started = made[:4], made[4:7], made[7:]
    axes = ("sta", "win")
    sent, other = [], None
    for index, targets in enumerate(rounds):
        args = [weight, *own, *started[index : index + 1]]
        args += [*other, sent[-1]] if index else [arriving, usable]
        *made, payload = kernel(
            functools.partial(cross_kernel, targets, not index, index < len(begun)),
            "cross_spectra",
            ([] if index else phasor_set) + [full_shape],
            [VMEM] * len(args),
        )(*args)
        other = other or made
        sent.append(payload)
    arrived = []
    for spectra, targets in zip(sent, rounds):
        moves = [(2 * b + w, 2 * targets[w][b] + w) for b in range(blocks) for w in range(2)]
        arrived.append(lax.ppermute(spectra, axes, moves))
    split = len(rounds) - 1
    def scratch(slots, lags):
        return [pltpu.VMEM((-(-slots // 8) * 8, lags), f32)] * 2 + [pltpu.VMEM((16, lags), f32)] * 2

    (split_table,) = kernel(
        functools.partial(split_table_kernel, blocks, rounds),
        "split_lag_table",
        [((split, 2, bins, LAGS), bf16)],
        [VMEM],
        scratch(split, LAGS),
    )(sent[-1])
    pairs, sums = rows * stations, []
    for slot in range(split):
        before, end = sums, slot == split - 1
        sums = kernel(
            functools.partial(sums_kernel, slot, half if end else 0),
            "split_lag_sums",
            [((pairs, half if end else LAGS), f32)],
            [VMEM] * (2 + len(sums)),
            flops=SMALL,
        )(split_table, arrived[slot], *sums)
    theirs = lax.ppermute(sums[0], "win", swap)
    own_spectra, whole_table = kernel(
        functools.partial(whole_table_kernel, blocks, rounds),
        "whole_lag_table",
        [full_shape, ((2, 2, bins, half), bf16)],
        [VMEM] * 10,
        scratch(2, half),
    )(weight, *own, *other, sums[0])
    (mine,) = kernel(
        functools.partial(mine_kernel, split - 1),
        "own_lag_sums",
        [((pairs, half), f32)],
        [VMEM] * 5,
        flops=SMALL,
    )(split_table, whole_table, arrived[split - 1], own_spectra, *before)
    (mine,) = kernel(
        functools.partial(sums_kernel, 0, 0),
        "last_lag_sums",
        [((pairs, half), f32)],
        [VMEM] * 3,
        flops=SMALL,
    )(whole_table, arrived[-1], mine)
    return (mine + theirs).reshape(rows, stations, half) * keep


def solution(mesh):
    return jax.shard_map(
        per_device,
        mesh=mesh,
        in_specs=(P(("days", "win"), "sta", None), P("days"), P(), P()),
        out_specs=P(("days", "sta"), None, "win"),
        check_vma=False,
    )
```

```python
import functools
import math

import jax
import jax.numpy as jnp
from jax import lax
from jax.experimental import pallas as pl
from jax.experimental.pallas import tpu as pltpu
from jax.sharding import PartitionSpec as P

LAGS = 512
BEGUN = 2
SMALL = 1000
ROUNDS = (
    ((3, 2, 6, 7, 5, 1, 0, 4), (4, 7, 5, 2, 1, 6, 3, 0)),
    ((6, 5, 7, 4, 0, 2, 1, 3), (7, 4, 1, 6, 3, 0, 5, 2)),
    ((1, 0, 4, 5, 7, 3, 2, 6), (5, 6, 3, 0, 2, 4, 7, 1)),
    ((2, 3, 0, 1, 6, 7, 4, 5), (2, 3, 0, 1, 6, 7, 4, 5)),
)
VMEM = pl.BlockSpec(memory_space=pltpu.VMEM)
ANY = pl.BlockSpec(memory_space=pl.ANY)
PARAMS = pltpu.CompilerParams(vmem_limit_bytes=48 * 1024 * 1024)

COS_COEF = (
    0.9999999890590218,
    -0.49999989101070386,
    0.041666489217381156,
    -0.001388780359807859,
    2.476988355752502e-05,
    -2.707903082088142e-07,
    1.724509174527214e-09,
)
SIN_COEF = (
    0.9999997571451633,
    -0.06534424613196173,
    0.001711441007161203,
    -2.461450561671638e-05,
    1.977699154629728e-07,
)


def cos_sin(angle):
    square = angle * angle
    cosine = COS_COEF[-1]
    for coef in COS_COEF[-2::-1]:
        cosine = cosine * square + coef
    sine = SIN_COEF[-1]
    for coef in SIN_COEF[-2::-1]:
        sine = sine * square + coef
    sine = sine * (angle - angle * square * (1.0 / math.pi**2))
    return cosine, sine


def rounds_of(blocks):
    if blocks == len(ROUNDS[0][0]):
        return ROUNDS
    steps = [(step, step ^ 1) for step in range(2, blocks, 2)] + [(1, 1)]
    return tuple(tuple(tuple(b ^ step for b in range(blocks)) for step in pair) for pair in steps)


def lookup(values, sta):
    found = jnp.int32(values[0])
    for b, value in enumerate(values[1:], 1):
        found = jnp.where(sta == b, value, found)
    return found


def peer(targets, sta, is_first):
    return jnp.where(is_first, lookup(targets[0], sta), lookup(targets[1], sta))


def sources(targets):
    return tuple(tuple(sorted(range(len(side)), key=lambda b: side[b])) for side in targets)


def in_hbm(array):
    return pltpu.with_memory_space_constraint(array, pltpu.HBM)


def position():
    return lax.axis_index("sta"), lax.axis_index("win")


def store_phasors(w, phase, usable, cos_ref, sin_ref, sum_ref, gap_ref):
    cosine, sine = cos_sin(phase.astype(jnp.float32))
    cosine = cosine.astype(jnp.bfloat16).astype(jnp.float32) * usable
    sine = sine.astype(jnp.bfloat16).astype(jnp.float32) * usable
    cos_ref[w] = cosine
    sin_ref[w] = sine
    sum_ref[w] = cosine + sine
    gap_ref[w] = cosine - sine


def prepare_kernel(blocks, begun, phase_hbm, valid_hbm, taper_hbm, mask_hbm, *refs):
    own, (usable_ref, weight_ref, keep_ref) = refs[:4], refs[4:7]
    begun_refs = refs[7 : 7 + len(begun)]
    phase_ref, valid_ref, taper_ref, mask_ref, sems = refs[7 + len(begun) :]
    sta, win = position()
    windows, stations, bins = phase_ref.shape
    rows = stations // blocks
    if taper_hbm.shape[1] > bins:
        taper_hbm = taper_hbm.at[:, pl.ds(pl.multiple_of(sta * bins, 128), bins)]
    copies = [
        pltpu.make_async_copy(source, target, sems.at[c])
        for c, (source, target) in enumerate(
            (
                (phase_hbm, phase_ref),
                (valid_hbm, valid_ref),
                (taper_hbm, taper_ref),
                (mask_hbm, mask_ref),
            )
        )
    ]
    for copy in copies:
        copy.start()
    for copy in copies[1:]:
        copy.wait()
    count = jnp.float32(0)
    for w in range(2 * windows):
        count += valid_ref[w].astype(jnp.float32)
    total = jnp.maximum(jnp.full((1, bins), count, jnp.float32), 1.0)
    weight_ref[...] = taper_ref[...] * (1.0 / jnp.sqrt(blocks * bins * total))
    for w in range(windows):
        usable = valid_ref[(1 - win) * windows + w].astype(jnp.float32)
        usable_ref[w] = jnp.full((1, bins), usable, jnp.float32)
    source = lax.broadcasted_iota(jnp.int32, keep_ref.shape[1:], 0)
    kept = jnp.zeros(keep_ref.shape[1:], jnp.float32)
    for block in range(blocks):
        kept = jnp.where(source // rows == block, mask_ref[sta, block].astype(jnp.float32), kept)
    for r in range(rows):
        keep_ref[r] = jnp.where(source == sta * rows + r, 0.0, kept)
    copies[0].wait()

    def phasors(w, carry):
        usable = valid_ref[win * windows + w].astype(jnp.float32)
        store_phasors(w, phase_ref[w], usable, *own)
        return carry

    lax.fori_loop(0, windows, phasors, 0, unroll=4)
    for targets, begun_ref in zip(begun, begun_refs):
        block = peer(targets, sta, win == 0)
        totals = add_full(start_full(rows, stations, bins), block, own)
        for r in range(rows):
            for part in range(3):
                begun_ref[r, part] = totals[r][part]


def add_full(totals, block, group):
    cos_ref, sin_ref, sum_ref, gap_ref = group
    rows = len(totals)

    def add(w, totals):
        cosine, plus, gap = cos_ref[w], sum_ref[w], gap_ref[w]
        added = []
        for r in range(rows):
            row = pl.ds(block * rows + r, 1)
            both, left, right = totals[r]
            added.append(
                (
                    both + sum_ref[w, row, :] * cosine,
                    left + sin_ref[w, row, :] * gap,
                    right + cos_ref[w, row, :] * plus,
                )
            )
        return added

    return lax.fori_loop(0, cos_ref.shape[0], add, totals, unroll=6)


def start_full(rows, stations, bins):
    return [(jnp.zeros((stations, bins), jnp.float32),) * 3] * rows


def full_sums(out_ref, block, own, other, weight, begun_ref=None):
    _, rows, stations, bins = out_ref.shape
    if begun_ref is None:
        totals = add_full(start_full(rows, stations, bins), block, own)
    else:
        totals = [tuple(begun_ref[r, part] for part in range(3)) for r in range(rows)]
    totals = add_full(totals, block, other)
    for r in range(rows):
        both, left, right = totals[r]
        out_ref[0, r] = ((both - left) * weight).astype(jnp.bfloat16).astype(out_ref.dtype)
        out_ref[1, r] = ((both - right) * weight).astype(jnp.bfloat16).astype(out_ref.dtype)


def other_kernel(phase_ref, usable_ref, *other):
    def phasors(w, carry):
        store_phasors(w, phase_ref[w], usable_ref[w], *other)
        return carry

    lax.fori_loop(0, phase_ref.shape[0], phasors, 0, unroll=12)


def cross_kernel(targets, first, begun, weight_ref, *refs):
    refs = list(refs)
    own, other = [refs.pop(0) for _ in range(4)], None
    begun_ref = refs.pop(0) if begun else None
    if first:
        phase_ref, usable_ref = refs.pop(0), refs.pop(0)
        other = [refs.pop(0) for _ in range(4)]
        other_kernel(phase_ref, usable_ref, *other)
    else:
        other = [refs.pop(0) for _ in range(4)]
    out_ref = refs[-1]
    sta, win = position()
    block = peer(targets, sta, win == 0)
    full_sums(out_ref, block, own, other, weight_ref[...], begun_ref)


def fill_tables(blocks, bands, table_ref, band_cos, band_sin, row_cos, row_sin):
    _, win = position()
    bins, columns = table_ref.shape[2:]
    wrap = 2 * blocks * bins
    half = LAGS // 2
    step = 16
    is_first = win == 0

    def lags(rows):
        column = lax.broadcasted_iota(jnp.int32, (rows, columns), 1)
        return jnp.where(is_first, column - half, jnp.where(column < half, column, column - LAGS))

    def phasor(index):
        wrapped = ((index + wrap // 2) & (wrap - 1)) - wrap // 2
        return cos_sin(wrapped.astype(jnp.float32) * (2.0 * math.pi / wrap))

    row = lax.broadcasted_iota(jnp.int32, (step, columns), 0)
    fine_cos, fine_sin = phasor(row * lags(step))
    band = lax.broadcasted_iota(jnp.int32, band_cos.shape, 0)
    first_bin = jnp.zeros(band_cos.shape, jnp.int32)
    for slot, block in enumerate(bands):
        first_bin = jnp.where(band == slot, block * bins, first_bin)
    band_cos[...], band_sin[...] = phasor(first_bin * lags(band_cos.shape[0]))
    steps = bins // step
    for start in range(0, steps, step):
        coarse_cos, coarse_sin = phasor((start + row) * step * lags(step))
        for slot in range(len(bands)):
            left_cos, left_sin = band_cos[slot : slot + 1, :], band_sin[slot : slot + 1, :]
            row_cos[...] = left_cos * coarse_cos - left_sin * coarse_sin
            row_sin[...] = -(left_sin * coarse_cos + left_cos * coarse_sin)

            def fill(a, carry, start=start, slot=slot):
                cosine, minus = row_cos[pl.ds(a, 1), :], row_sin[pl.ds(a, 1), :]
                place = pl.ds(pl.multiple_of((start + a) * step, step), step)
                value = cosine * fine_cos + minus * fine_sin
                table_ref[slot, 0, place, :] = value.astype(jnp.bfloat16)
                value = minus * fine_cos - cosine * fine_sin
                table_ref[slot, 1, place, :] = value.astype(jnp.bfloat16)
                return carry

            lax.fori_loop(0, min(step, steps - start), fill, 0, unroll=4)


def split_table_kernel(blocks, rounds, after_ref, table_ref, *scratch):
    sta, win = position()
    bands = [peer(sources(targets), sta, win == 0) for targets in rounds[:-1]]
    fill_tables(blocks, bands, table_ref, *scratch)


def whole_table_kernel(blocks, rounds, weight_ref, *refs):
    own, other, (after_ref, own_ref, table_ref, *scratch) = refs[:4], refs[4:8], refs[8:]
    sta, win = position()
    bands = [peer(sources(rounds[-1]), sta, win == 0), sta]
    fill_tables(blocks, bands, table_ref, *scratch)
    full_sums(own_ref, sta, own, other, weight_ref[...])


def times(spectra_ref, table_ref, slot, lags):
    _, rows, stations, bins = spectra_ref.shape
    total = 0.0
    for c in range(2):
        spectra = spectra_ref[c].reshape(rows * stations, bins)
        table = table_ref[slot, c, :, lags]
        total = total + jnp.dot(spectra, table, preferred_element_type=jnp.float32)
    return total


def sums_kernel(slot, first_lag, table_ref, spectra_ref, *refs):
    *before, out_ref = refs
    lags = pl.ds(first_lag, out_ref.shape[-1])
    total = times(spectra_ref, table_ref, slot, lags)
    for before_ref in before:
        total = total + before_ref[:, lags]
    out_ref[...] = total


def mine_kernel(slot, split_ref, whole_ref, spectra_ref, own_ref, before_ref, out_ref):
    lags = pl.ds(0, out_ref.shape[-1])
    total = before_ref[:, lags] + times(spectra_ref, split_ref, slot, lags)
    out_ref[...] = total + times(own_ref, whole_ref, 1, lags)


def per_device(phases, window_valid, freq_taper, pair_mask):
    blocks = lax.axis_size("sta")
    windows, bins, stations = phases.shape
    rows = stations // blocks
    half = LAGS // 2
    rounds = rounds_of(blocks)
    swap = [(0, 1), (1, 0)]

    def kernel(body, name, outs, ins, scratch=(), flops=None):
        return pl.pallas_call(
            body,
            out_shape=[jax.ShapeDtypeStruct(shape, dtype) for shape, dtype in outs],
            in_specs=ins,
            out_specs=[VMEM] * len(outs),
            scratch_shapes=list(scratch),
            compiler_params=PARAMS,
            cost_estimate=flops and pl.CostEstimate(flops=flops, bytes_accessed=1000, transcendentals=0),
            name=name,
        )

    f32, bf16 = jnp.float32, jnp.bfloat16
    phasor_set = [((windows, stations, bins), f32)] * 4
    full_shape = ((2, rows, stations, bins), bf16)
    half_shape = ((rows, stations, half), f32)
    phases = jnp.transpose(phases, (0, 2, 1))
    arriving = lax.ppermute(phases, "win", swap)
    taper = freq_taper
    if bins % 128:
        taper = lax.dynamic_slice_in_dim(freq_taper, lax.axis_index("sta") * bins, bins)
    begun = rounds[:BEGUN]
    made = kernel(
        functools.partial(prepare_kernel, blocks, begun),
        "own_phasors",
        phasor_set
        + [((windows, 1, bins), f32), ((1, bins), f32), half_shape]
        + [((rows, 3, stations, bins), f32)] * len(begun),
        [ANY] * 4,
        [
            pltpu.VMEM((windows, stations, bins), bf16),
            pltpu.SMEM(window_valid.shape, jnp.int32),
            pltpu.VMEM((1, bins), f32),
            pltpu.SMEM(pair_mask.shape, jnp.int32),
            pltpu.SemaphoreType.DMA((4,)),
        ],
    )(*(in_hbm(array) for array in (phases, window_valid, taper.reshape(1, -1), pair_mask)))
    own, (usable, weight, keep), started = made[:4], made[4:7], made[7:]
    axes = ("sta", "win")
    sent, other = [], None
    for index, targets in enumerate(rounds):
        args = [weight, *own, *started[index : index + 1]]
        args += [*other, sent[-1]] if index else [arriving, usable]
        *made, payload = kernel(
            functools.partial(cross_kernel, targets, not index, index < len(begun)),
            "cross_spectra",
            ([] if index else phasor_set) + [full_shape],
            [VMEM] * len(args),
        )(*args)
        other = other or made
        sent.append(payload)
    arrived = []
    for spectra, targets in zip(sent, rounds):
        moves = [(2 * b + w, 2 * targets[w][b] + w) for b in range(blocks) for w in range(2)]
        arrived.append(lax.ppermute(spectra, axes, moves))
    split = len(rounds) - 1
    def scratch(slots, lags):
        return [pltpu.VMEM((-(-slots // 8) * 8, lags), f32)] * 2 + [pltpu.VMEM((16, lags), f32)] * 2

    (split_table,) = kernel(
        functools.partial(split_table_kernel, blocks, rounds),
        "split_lag_table",
        [((split, 2, bins, LAGS), bf16)],
        [VMEM],
        scratch(split, LAGS),
    )(sent[-1])
    pairs, sums = rows * stations, []
    for slot in range(split):
        before, end = sums, slot == split - 1
        sums = kernel(
            functools.partial(sums_kernel, slot, half if end else 0),
            "split_lag_sums",
            [((pairs, half if end else LAGS), f32)],
            [VMEM] * (2 + len(sums)),
            flops=SMALL,
        )(split_table, arrived[slot], *sums)
    theirs = lax.ppermute(sums[0], "win", swap)
    own_spectra, whole_table = kernel(
        functools.partial(whole_table_kernel, blocks, rounds),
        "whole_lag_table",
        [full_shape, ((2, 2, bins, half), bf16)],
        [VMEM] * 10,
        scratch(2, half),
    )(weight, *own, *other, sums[0])
    (mine,) = kernel(
        functools.partial(mine_kernel, split - 1),
        "own_lag_sums",
        [((pairs, half), f32)],
        [VMEM] * 5,
        flops=SMALL,
    )(split_table, whole_table, arrived[split - 1], own_spectra, *before)
    (mine,) = kernel(
        functools.partial(sums_kernel, 0, 0),
        "last_lag_sums",
        [((pairs, half), f32)],
        [VMEM] * 3,
        flops=SMALL,
    )(whole_table, arrived[-1], mine)
    return (mine + theirs).reshape(rows, stations, half) * keep


def solution(mesh):
    return jax.shard_map(
        per_device,
        mesh=mesh,
        in_specs=(P(("days", "win"), "sta", None), P("days"), P(), P()),
        out_specs=P(("days", "sta"), None, "win"),
        check_vma=False,
    )
```
